32 devices in a mesh: ctx: 8 (over z, y), head: 4 (over x, core).
Axes of the slice: x: 2, y: 2, z: 4, core: 2. Of those that a mesh axis runs over, the one named last changes fastest.
Arguments:
- tokens: bfloat16 [2048, 1024], P('ctx', 'head')
- gain: float32 [1024], replicated, may hold values from 0.25 to 1.75
- w_query: bfloat16 [1024, 1024], P(None, 'head'), may hold values from -0.1875 to 0.1875
- w_key: bfloat16 [1024, 1024], P(None, 'head'), may hold values from -0.1875 to 0.1875
- w_value: bfloat16 [1024, 1024], P(None, 'head'), may hold values from -0.1875 to 0.1875
- w_out: bfloat16 [1024, 1024], P('head'), may hold values from -0.1875 to 0.1875
- temper: float32 [16], P('head'), may hold values from 4 to 12
- adjacency: int32 [16, 16], replicated, may hold values from 0 to 1, as said below
- order: int32 [16], replicated, may hold values from 0 to 15, each once
Outputs:
- update: bfloat16 [2048, 1024], P('ctx', 'head')
The draws below stay inside these ranges and needn't reach their ends.
Inputs may be any that keep to these rules, and one draw needn't show every extreme that they name: Entries are 0 or 1; adjacency[a][a] is 1 for every compartment block a. `order`: each compartment block appears once.
All inputs are finite; a program needn't handle non-finite values.
Results may differ from the reference program's by a relative error of at most 0.015.
Values may be sent and summed in bfloat16 or wider, within the bound.
A program may use at most 64 MiB of HBM per device.

```python
import math
import jax
import jax.numpy as jnp
from jax import lax

D = 1024
H = 16
HD = 64
BLOCK = 128
TOKENS = 2048
NB = 16


def draw_tokens(key, part):
    first, second, third = jax.random.split(key, 3)
    base = jnp.clip(jax.random.normal(first, (TOKENS, D), jnp.float32), -6.0, 6.0)
    row_scale = jnp.exp(jax.random.uniform(second, (TOKENS, 1), jnp.float32, 0.0, math.log(10.0)))
    col_scale = jnp.exp(jax.random.uniform(third, (1, D), jnp.float32, 0.0, math.log(10.0)))
    return (0.1 * base * row_scale * col_scale).astype(jnp.bfloat16)


def draw_adjacency(key, part):
    first, second = jax.random.split(jax.random.fold_in(key, 7))
    blocks = TOKENS // BLOCK
    reach = jax.random.randint(first, (blocks, 1), 0, blocks // 2 + 1)
    rows = jnp.arange(blocks, dtype=jnp.int32)[:, None]
    cols = jnp.arange(blocks, dtype=jnp.int32)[None, :]
    near = jnp.abs(rows - cols) <= reach
    extra = jax.random.randint(second, (blocks, blocks), 0, 16) == 0
    return (near | extra).astype(jnp.int32)


def steps_of(key, dims, cuts, low, top_value):
    factor_of, own = 1.0, jax.random.fold_in(key, 6)
    for axis_at, shards_of in cuts:
        steps = jnp.exp(jax.random.uniform(jax.random.fold_in(own, axis_at), (shards_of,), jnp.float32, low / len(cuts), top_value / len(cuts)))
        factor_of = factor_of * jnp.repeat(steps, dims[axis_at] // shards_of).reshape([-1 if axis == axis_at else 1 for axis in range(len(dims))])
    return factor_of


def centred(stream_key, extent, spread, most, shards=(), kind=jnp.bfloat16):
    values = jax.random.normal(stream_key, extent, jnp.float32) * spread
    if len(shards) > 0:
        values = steps_of(stream_key, extent, shards, -0.22, 0.18) * values
    return jnp.clip(values, min=-most, max=most).astype(kind)


def setup_inputs(seed: int = 0) -> dict:
    arg_keys = jax.random.split(jax.random.key(seed), 10)
    return {
        "tokens": draw_tokens(jax.random.fold_in(arg_keys[9], 71), 0),
        "gain": jnp.clip(1.0 + 0.15 * jax.random.normal(arg_keys[1], (D,), jnp.float32), 0.25, 1.75),
        "w_query": centred(arg_keys[2], (D, H * HD), D ** -0.5, 0.1875, ((1, 4),)),
        "w_key": centred(arg_keys[3], (D, H * HD), D ** -0.5, 0.1875, ((1, 4),)),
        "w_value": centred(arg_keys[4], (D, H * HD), D ** -0.5, 0.1875, ((1, 4),)),
        "w_out": centred(arg_keys[5], (H * HD, D), (H * HD) ** -0.5, 0.1875, ((0, 4),)),
        "temper": jnp.clip(jnp.exp(math.log(12.0) - 1.0986123 * jax.random.uniform(arg_keys[6], (H,), jnp.float32) ** steps_of(arg_keys[6], (H,), ((0, 4),), -0.2, 0.2)), 4.0, 12.0),
        "adjacency": draw_adjacency(jax.random.fold_in(arg_keys[9], 71), 0),
        "order": jax.random.permutation(arg_keys[8], NB).astype(jnp.int32),
    }


def normalize(values):
    return values * lax.rsqrt(lax.optimization_barrier(jnp.mean(values * values, axis=-1, keepdims=True)) + 1e-06)

def reference(tokens, gain, w_query, w_key, w_value, w_out, temper, adjacency, order):
    total_rows = tokens.shape[0]
    normed = (normalize(tokens.astype(jnp.float32)) * gain).astype(jnp.bfloat16)
    query = normalize(jnp.dot(normed, w_query, preferred_element_type=jnp.float32).reshape(total_rows, H, HD))
    query = (query * (temper[None, :, None] / HD)).astype(jnp.bfloat16)
    keys = normalize(jnp.dot(normed, w_key, preferred_element_type=jnp.float32).reshape(total_rows, H, HD)).astype(jnp.bfloat16)
    values = jnp.dot(normed, w_value, preferred_element_type=jnp.float32).astype(jnp.bfloat16).reshape(total_rows, H, HD)
    linked = adjacency[order][:, order]
    keys_wide = keys.astype(jnp.float32)
    values_wide = values.astype(jnp.float32)

    def one_block(index):
        start = index * BLOCK
        block_query = lax.dynamic_slice_in_dim(query, start, BLOCK, 0).astype(jnp.float32)
        allowed = jnp.repeat(linked[index], BLOCK) > 0
        scores = jnp.einsum('qhd,khd->hqk', block_query, keys_wide)
        probs = jnp.where(allowed[None, None, :], jnp.exp(scores), 0.0)
        weight = lax.optimization_barrier(jnp.sum(probs, axis=-1))
        rounded = lax.optimization_barrier(probs.astype(jnp.bfloat16)).astype(jnp.float32)
        summed = jnp.einsum('hqk,khd->qhd', rounded, values_wide)
        return (summed / weight.T[:, :, None]).astype(jnp.bfloat16)
    attended = lax.map(one_block, jnp.arange(total_rows // BLOCK, dtype=jnp.int32))
    attended = attended.reshape(total_rows, H * HD)
    return jnp.dot(attended, w_out, preferred_element_type=jnp.float32).astype(jnp.bfloat16)
```

```python
import functools

import jax
import jax.numpy as jnp
from jax import lax
from jax.experimental import pallas as pl
from jax.experimental.pallas import tpu as pltpu
from jax.sharding import PartitionSpec as P

BLOCK = 128
CHUNKS = 2
EPS = 1e-06
MESH = pl.DeviceIdType.MESH
F32 = jnp.float32
BF16 = jnp.bfloat16


def visit(line, depth, k):
    far = depth - 1 - line
    near = jnp.minimum(line, far)
    both = jnp.where(k % 2 == 1, line - (k + 1) // 2, line + k // 2)
    rest = jnp.where(line < far, line + (k - near), line - (k - near))
    return jnp.where(k <= 2 * near, both, rest)


def kernel(
    depth,
    order_ref, adj_ref, temper_ref, gain_ref, tokens_ref, wq_hbm, wk_hbm, wv_hbm, wo_hbm,
    out_ref,
    tok, wq, wk, wv, wo, mean_mat, kvh, kvr, qh, qr, qm, acc, asend, abuf, part, csend, crecv, xsend, xrecv,
    w_sem, t_sem, zs, zr, xs, xr, cs, cr, ys, yr, qs, qrs, as_, ar, ocs, ocr, oxs, oxr,
):
    ctx, head = lax.axis_index("ctx"), lax.axis_index("head")
    line, y = ctx // 2, ctx % 2
    x, c = head // 2, head % 2
    oy, ox, oc = 1 - y, 1 - x, 1 - c
    rows, cols = tokens_ref.shape
    heads = temper_ref.shape[0]
    width = wq.shape[1]
    size = width // heads
    pair = width // 2
    rp = rows // CHUNKS
    total = depth * CHUNKS
    features = wq.shape[0]
    lag = CHUNKS + 1
    has_left, has_right = line > 0, line < depth - 1
    at_left, at_right = (ctx - 2, head), (ctx + 2, head)
    at_y = (line * 2 + oy, head)
    at_x = (ctx, ox * 2 + c)
    at_c = (ctx, x * 2 + oc)
    xhead = ox * 2 + c
    chead = x * 2 + oc
    dhead = ox * 2 + oc

    def remote(src, dst, send, recv, where):
        return pltpu.make_async_remote_copy(
            src_ref=src, dst_ref=dst, send_sem=send, recv_sem=recv, device_id=where, device_id_type=MESH
        )

    loads = [
        pltpu.make_async_copy(wk_hbm, wk, w_sem.at[0]),
        pltpu.make_async_copy(wv_hbm, wv, w_sem.at[1]),
        pltpu.make_async_copy(wq_hbm, wq, w_sem.at[2]),
    ]
    count = wo.shape[0]
    for h in range(count):
        loads.append(pltpu.make_async_copy(wo_hbm.at[:, pl.ds(h * cols, cols)], wo.at[h], w_sem.at[3 + h]))
    own = [
        pltpu.make_async_copy(tokens_ref.at[pl.ds(j * rp, rp), :], tok.at[line * CHUNKS + j, head], t_sem.at[j])
        for j in range(CHUNKS)
    ]
    for copy in own + loads:
        copy.start()

    barrier = pltpu.get_barrier_semaphore()
    for where in (at_y, at_x, at_c):
        pl.semaphore_signal(barrier, inc=1, device_id=where, device_id_type=MESH)

    @pl.when(has_left)
    def _():
        pl.semaphore_signal(barrier, inc=1, device_id=at_left, device_id_type=MESH)

    @pl.when(has_right)
    def _():
        pl.semaphore_signal(barrier, inc=1, device_id=at_right, device_id_type=MESH)

    row_id = lax.broadcasted_iota(jnp.int32, (width, width), 0) // size
    col_id = lax.broadcasted_iota(jnp.int32, (width, width), 1) // size
    mean_mat[...] = jnp.where(row_id == col_id, 1.0 / size, 0.0).astype(BF16)
    acc[...] = jnp.zeros_like(acc)
    pl.semaphore_wait(barrier, 3 + has_left.astype(jnp.int32) + has_right.astype(jnp.int32))

    def slot_of(n):
        origin = visit(line, depth, n // CHUNKS)
        return origin, origin * CHUNKS + n % CHUNKS

    def z_right(s):
        return remote(tok.at[s, head], tok.at[s, head], zs.at[1, s], zr.at[s], at_right)

    def z_left(s):
        return remote(tok.at[s, head], tok.at[s, head], zs.at[0, s], zr.at[s], at_left)

    def x_copy(s, h):
        return remote(tok.at[s, h], tok.at[s, h], xs.at[s], xr.at[s], at_x)

    def c_copy(s, h, which):
        return remote(tok.at[s, h], tok.at[s, h], cs.at[s, which], cr.at[s, which], at_c)

    def y_copy(s):
        return remote(kvh.at[s, oy], kvr.at[s], ys.at[s], yr.at[s], at_y)

    def q_copy(j):
        return remote(qh.at[oy, j], qr.at[j], qs.at[j], qrs.at[j], at_y)

    def spread(origin, s):
        @pl.when(jnp.logical_and(has_right, origin <= line))
        def _():
            z_right(s).start()

        @pl.when(jnp.logical_and(has_left, origin >= line))
        def _():
            z_left(s).start()

        x_copy(s, head).start()
        c_copy(s, head, 0).start()

    for j in range(CHUNKS):
        own[j].wait()
        spread(line, line * CHUNKS + j)
    for copy in loads:
        copy.wait()

    def unit(values):
        mean = jnp.dot((values * values).astype(BF16), mean_mat[...], preferred_element_type=F32)
        return values * lax.rsqrt(mean + EPS)

    lane_w = lax.broadcasted_iota(jnp.int32, (1, width), 1) // size
    scale = jnp.zeros((1, width), F32)
    for h in range(heads):
        scale = jnp.where(lane_w == h, temper_ref[h] / size, scale)

    def project(n):
        origin, s = slot_of(n)
        c_copy(s, chead, 0).wait_recv()
        c_copy(s, dhead, 1).wait_recv()
        parts = [tok[s, h].astype(F32) for h in range(count)]
        squares = parts[0] * parts[0]
        for p in parts[1:]:
            squares = squares + p * p
        inv = lax.rsqrt(jnp.sum(squares, axis=-1, keepdims=True) * (1.0 / features) + EPS)
        normed = jnp.concatenate(
            [(parts[h] * inv * gain_ref[:, h * cols:(h + 1) * cols]).astype(BF16) for h in range(count)], axis=1
        )
        keys = unit(jnp.dot(normed, wk[...], preferred_element_type=F32)).astype(BF16)
        values = jnp.dot(normed, wv[...], preferred_element_type=F32).astype(BF16)
        for half in range(2):
            kvh[s, half, 0] = keys[:, half * pair:(half + 1) * pair]
            kvh[s, half, 1] = values[:, half * pair:(half + 1) * pair]
        y_copy(s).start()

        @pl.when(n < CHUNKS)
        def _():
            query = unit(jnp.dot(normed, wq[...], preferred_element_type=F32))
            query = (query * scale).astype(BF16)
            for half in range(2):
                qh[half, n] = query[:, half * pair:(half + 1) * pair]
            q_copy(n).start()

    low = lax.broadcasted_iota(jnp.int32, (1, pair), 1) < size

    def split_queries():
        for j in range(CHUNKS):
            q_copy(j).wait_recv()
        for side in range(2):
            for j in range(CHUNKS):
                piece = qh[y, j] if side == 0 else qr[j]
                at = side * rows + j * rp
                zero = jnp.zeros_like(piece)
                qm[0, at:at + rp, :] = jnp.where(low, piece, zero)
                qm[1, at:at + rp, :] = jnp.where(low, zero, piece)

    local = rows // BLOCK
    per_chunk = rp // BLOCK
    q_blocks = [order_ref[(line * 2 + side) * local + i] for side in (y, oy) for i in range(local)]
    key_lane = lax.broadcasted_iota(jnp.int32, (1, 2 * rp), 1) // BLOCK

    def attend(n):
        origin, s = slot_of(n)
        y_copy(s).wait_recv()
        keys = jnp.concatenate([kvh[s, y, 0], kvr[s, 0]], axis=0)
        values = jnp.concatenate([kvh[s, y, 1], kvr[s, 1]], axis=0)
        first = (n % CHUNKS) * per_chunk
        k_blocks = [order_ref[(origin * 2 + side) * local + first + i] for side in (y, oy) for i in range(per_chunk)]
        masks = []
        for qb in q_blocks:
            mask = jnp.zeros((1, 2 * rp), F32)
            for i, kb in enumerate(k_blocks):
                mask = jnp.where(key_lane == i, (adj_ref[qb, kb] > 0).astype(F32), mask)
            masks.append(mask)
        ones = jnp.ones_like(values)
        for h in range(2):
            mine = jnp.where(low, values, ones) if h == 0 else jnp.where(low, ones, values)
            scores = lax.dot_general(qm[h], keys, (((1,), (1,)), ((), ())), preferred_element_type=F32)
            probs = jnp.concatenate(
                [(jnp.exp(scores[i * BLOCK:(i + 1) * BLOCK]) * masks[i]).astype(BF16) for i in range(2 * local)], axis=0
            )
            acc[h] += jnp.dot(probs, mine, preferred_element_type=F32)

    def step(n, carry):
        @pl.when(n + CHUNKS < total)
        def _():
            origin, s = slot_of(n + CHUNKS)
            z_left(s).wait_recv()
            spread(origin, s)

        @pl.when(n < total)
        def _():
            origin, s = slot_of(n)
            x_copy(s, xhead).wait_recv()
            c_copy(s, xhead, 1).start()

        @pl.when(jnp.logical_and(n >= 1, n <= total))
        def _():
            project(n - 1)

        @pl.when(n == lag)
        def _():
            split_queries()

        @pl.when(n >= lag)
        def _():
            attend(n - lag)

        return carry

    lax.fori_loop(0, total + lag, step, 0)

    top = jnp.where(low, acc[0], acc[1])
    weight = pltpu.roll(jnp.where(low, acc[1], acc[0]), size, 1)
    attended = (top / weight).astype(BF16)
    asend[...] = attended[rows:]
    a_copy = remote(asend, abuf.at[y], as_, ar, at_y)
    a_copy.start()
    abuf[y] = attended[:rows]
    remote(asend, abuf.at[oy], as_, ar, at_y).wait_recv()

    c_outs, x_outs = [], []
    for r in range(CHUNKS):
        at = r * rp
        feats = jnp.concatenate([abuf[0, at:at + rp, :], abuf[1, at:at + rp, :]], axis=1)
        csend[r, 0] = jnp.dot(feats, wo[dhead], preferred_element_type=F32).astype(BF16)
        csend[r, 1] = jnp.dot(feats, wo[chead], preferred_element_type=F32).astype(BF16)
        c_out = remote(csend.at[r], crecv.at[r], ocs.at[r], ocr.at[r], at_c)
        c_out.start()
        c_outs.append(c_out)
        part[r, 0] = jnp.dot(feats, wo[xhead], preferred_element_type=F32)
        part[r, 1] = jnp.dot(feats, wo[head], preferred_element_type=F32)
    for r in range(CHUNKS):
        c_outs[r].wait_recv()
        xsend[r] = (part[r, 0] + crecv[r, 0].astype(F32)).astype(BF16)
        x_out = remote(xsend.at[r], xrecv.at[r], oxs.at[r], oxr.at[r], at_x)
        x_out.start()
        x_outs.append(x_out)
    for r in range(CHUNKS):
        x_outs[r].wait_recv()
        whole = part[r, 1] + crecv[r, 1].astype(F32) + xrecv[r].astype(F32)
        out_ref[r * rp:(r + 1) * rp, :] = whole.astype(BF16)

    def drain(n, carry):
        origin, s = slot_of(n)

        @pl.when(jnp.logical_and(has_right, origin <= line))
        def _():
            z_right(s).wait_send()

        @pl.when(jnp.logical_and(has_left, origin >= line))
        def _():
            z_left(s).wait_send()

        x_copy(s, head).wait_send()
        c_copy(s, head, 0).wait_send()
        c_copy(s, xhead, 1).wait_send()
        y_copy(s).wait_send()
        return carry

    lax.fori_loop(0, total, drain, 0)
    for j in range(CHUNKS):
        q_copy(j).wait_send()
        c_outs[j].wait_send()
        x_outs[j].wait_send()
    a_copy.wait_send()


def shards(depth, tokens, gain, w_query, w_key, w_value, w_out, temper, adjacency, order):
    rows, cols = tokens.shape
    features, width = w_query.shape
    count = features // cols
    pair = width // 2
    rp = rows // CHUNKS
    total = depth * CHUNKS
    dma = pltpu.SemaphoreType.DMA
    smem = pl.BlockSpec(memory_space=pltpu.SMEM)
    vmem = pl.BlockSpec(memory_space=pltpu.VMEM)
    hbm = pl.BlockSpec(memory_space=pl.ANY)
    return pl.pallas_call(
        functools.partial(kernel, depth),
        out_shape=jax.ShapeDtypeStruct((rows, cols), BF16),
        in_specs=[smem, smem, smem, vmem, hbm, hbm, hbm, hbm, hbm],
        out_specs=vmem,
        scratch_shapes=[
            pltpu.VMEM((total, count, rp, cols), BF16),
            pltpu.VMEM((features, width), BF16),
            pltpu.VMEM((features, width), BF16),
            pltpu.VMEM((features, width), BF16),
            pltpu.VMEM((count, width, cols), BF16),
            pltpu.VMEM((width, width), BF16),
            pltpu.VMEM((total, 2, 2, rp, pair), BF16),
            pltpu.VMEM((total, 2, rp, pair), BF16),
            pltpu.VMEM((2, CHUNKS, rp, pair), BF16),
            pltpu.VMEM((CHUNKS, rp, pair), BF16),
            pltpu.VMEM((2, 2 * rows, pair), BF16),
            pltpu.VMEM((2, 2 * rows, pair), F32),
            pltpu.VMEM((rows, pair), BF16),
            pltpu.VMEM((2, rows, pair), BF16),
            pltpu.VMEM((CHUNKS, 2, rp, cols), F32),
            pltpu.VMEM((CHUNKS, 2, rp, cols), BF16),
            pltpu.VMEM((CHUNKS, 2, rp, cols), BF16),
            pltpu.VMEM((CHUNKS, rp, cols), BF16),
            pltpu.VMEM((CHUNKS, rp, cols), BF16),
            dma((3 + count,)),
            dma((CHUNKS,)),
            dma((2, total)),
            dma((total,)),
            dma((total,)),
            dma((total,)),
            dma((total, 2)),
            dma((total, 2)),
            dma((total,)),
            dma((total,)),
            dma((CHUNKS,)),
            dma((CHUNKS,)),
            dma,
            dma,
            dma((CHUNKS,)),
            dma((CHUNKS,)),
            dma((CHUNKS,)),
            dma((CHUNKS,)),
        ],
        compiler_params=pltpu.CompilerParams(
            collective_id=0, has_side_effects=True, vmem_limit_bytes=56 * 1024 * 1024
        ),
    )(order, adjacency, temper, gain.reshape(1, features), tokens, w_query, w_key, w_value, w_out)


def solution(mesh):
    in_specs = (
        P("ctx", "head"),
        P(),
        P(None, "head"),
        P(None, "head"),
        P(None, "head"),
        P("head", None),
        P("head"),
        P(),
        P(),
    )
    out_specs = P("ctx", "head")
    body = functools.partial(shards, mesh.shape["ctx"] // 2)
    return jax.shard_map(body, mesh=mesh, in_specs=in_specs, out_specs=out_specs, check_vma=False)
```

```python
import functools

import jax
import jax.numpy as jnp
from jax import lax
from jax.experimental import pallas as pl
from jax.experimental.pallas import tpu as pltpu
from jax.sharding import PartitionSpec as P

BLOCK = 128
CHUNKS = 2
EPS = 1e-06
MESH = pl.DeviceIdType.MESH
F32 = jnp.float32
BF16 = jnp.bfloat16


def visit(line, depth, n):
    far = depth - 1 - line
    near = jnp.minimum(line, far) * CHUNKS
    p = n - CHUNKS
    paired = p < 2 * near
    t = jnp.where(paired, p // 2, p - near)
    to_left = jnp.where(paired, p % 2 == 0, line > far)
    away = t // CHUNKS + 1
    origin = jnp.where(n < CHUNKS, line, jnp.where(to_left, line - away, line + away))
    return origin, jnp.where(n < CHUNKS, n, t % CHUNKS)


def kernel(
    depth,
    order_ref, adj_ref, temper_ref, gain_ref, tokens_ref, wq_hbm, wk_hbm, wv_hbm, wo_hbm,
    out_ref,
    tok, wq, wk, wv, wo, mean_mat, kvh, kvr, qh, qr, qm, acc, asend, abuf, part, csend, crecv, xsend, xrecv,
    w_sem, t_sem, zs, zr, xs, xr, cs, cr, ys, yr, qs, qrs, as_, ar, ocs, ocr, oxs, oxr,
):
    ctx, head = lax.axis_index("ctx"), lax.axis_index("head")
    line, y = ctx // 2, ctx % 2
    x, c = head // 2, head % 2
    oy, ox, oc = 1 - y, 1 - x, 1 - c
    rows, cols = tokens_ref.shape
    heads = temper_ref.shape[0]
    width = wq.shape[1]
    size = width // heads
    pair = width // 2
    rp = rows // CHUNKS
    total = depth * CHUNKS
    features = wq.shape[0]
    lag = CHUNKS + 1
    has_left, has_right = line > 0, line < depth - 1
    at_left, at_right = (ctx - 2, head), (ctx + 2, head)
    at_y = (line * 2 + oy, head)
    at_x = (ctx, ox * 2 + c)
    at_c = (ctx, x * 2 + oc)
    xhead = ox * 2 + c
    chead = x * 2 + oc
    dhead = ox * 2 + oc

    def remote(src, dst, send, recv, where):
        return pltpu.make_async_remote_copy(
            src_ref=src, dst_ref=dst, send_sem=send, recv_sem=recv, device_id=where, device_id_type=MESH
        )

    loads = [
        pltpu.make_async_copy(wk_hbm, wk, w_sem.at[0]),
        pltpu.make_async_copy(wv_hbm, wv, w_sem.at[1]),
        pltpu.make_async_copy(wq_hbm, wq, w_sem.at[2]),
    ]
    count = wo.shape[0]
    for h in range(count):
        loads.append(pltpu.make_async_copy(wo_hbm.at[:, pl.ds(h * cols, cols)], wo.at[h], w_sem.at[3 + h]))
    own = [
        pltpu.make_async_copy(tokens_ref.at[pl.ds(j * rp, rp), :], tok.at[line * CHUNKS + j, head], t_sem.at[j])
        for j in range(CHUNKS)
    ]
    for copy in own + loads:
        copy.start()

    barrier = pltpu.get_barrier_semaphore()
    for where in (at_y, at_x, at_c):
        pl.semaphore_signal(barrier, inc=1, device_id=where, device_id_type=MESH)

    @pl.when(has_left)
    def _():
        pl.semaphore_signal(barrier, inc=1, device_id=at_left, device_id_type=MESH)

    @pl.when(has_right)
    def _():
        pl.semaphore_signal(barrier, inc=1, device_id=at_right, device_id_type=MESH)

    row_id = lax.broadcasted_iota(jnp.int32, (width, width), 0) // size
    col_id = lax.broadcasted_iota(jnp.int32, (width, width), 1) // size
    mean_mat[...] = jnp.where(row_id == col_id, 1.0 / size, 0.0).astype(BF16)
    acc[...] = jnp.zeros_like(acc)
    pl.semaphore_wait(barrier, 3 + has_left.astype(jnp.int32) + has_right.astype(jnp.int32))

    def slot_of(n):
        origin, j = visit(line, depth, n)
        return origin, origin * CHUNKS + j

    def z_right(s):
        return remote(tok.at[s, head], tok.at[s, head], zs.at[1, s], zr.at[s], at_right)

    def z_left(s):
        return remote(tok.at[s, head], tok.at[s, head], zs.at[0, s], zr.at[s], at_left)

    def x_copy(s, h):
        return remote(tok.at[s, h], tok.at[s, h], xs.at[s], xr.at[s], at_x)

    def c_copy(s, h, which):
        return remote(tok.at[s, h], tok.at[s, h], cs.at[s, which], cr.at[s, which], at_c)

    def y_copy(s):
        return remote(kvh.at[s, oy], kvr.at[s], ys.at[s], yr.at[s], at_y)

    def q_copy(j):
        return remote(qh.at[oy, j], qr.at[j], qs.at[j], qrs.at[j], at_y)

    def spread(origin, s):
        @pl.when(jnp.logical_and(has_right, origin <= line))
        def _():
            z_right(s).start()

        @pl.when(jnp.logical_and(has_left, origin >= line))
        def _():
            z_left(s).start()

        x_copy(s, head).start()
        c_copy(s, head, 0).start()

    for j in range(CHUNKS):
        own[j].wait()
        spread(line, line * CHUNKS + j)
    for copy in loads[:3]:
        copy.wait()

    def unit(values):
        mean = jnp.dot((values * values).astype(BF16), mean_mat[...], preferred_element_type=F32)
        return values * lax.rsqrt(mean + EPS)

    lane_w = lax.broadcasted_iota(jnp.int32, (1, width), 1) // size
    scale = jnp.zeros((1, width), F32)
    for h in range(heads):
        scale = jnp.where(lane_w == h, temper_ref[h] / size, scale)

    def project(n):
        origin, s = slot_of(n)
        c_copy(s, chead, 0).wait_recv()
        c_copy(s, dhead, 1).wait_recv()
        parts = [tok[s, h].astype(F32) for h in range(count)]
        squares = parts[0] * parts[0]
        for p in parts[1:]:
            squares = squares + p * p
        inv = lax.rsqrt(jnp.sum(squares, axis=-1, keepdims=True) * (1.0 / features) + EPS)
        normed = jnp.concatenate(
            [(parts[h] * inv * gain_ref[:, h * cols:(h + 1) * cols]).astype(BF16) for h in range(count)], axis=1
        )
        keys = unit(jnp.dot(normed, wk[...], preferred_element_type=F32)).astype(BF16)
        values = jnp.dot(normed, wv[...], preferred_element_type=F32).astype(BF16)
        for half in range(2):
            kvh[s, half, 0] = keys[:, half * pair:(half + 1) * pair]
            kvh[s, half, 1] = values[:, half * pair:(half + 1) * pair]
        y_copy(s).start()

        @pl.when(n < CHUNKS)
        def _():
            query = unit(jnp.dot(normed, wq[...], preferred_element_type=F32))
            query = (query * scale).astype(BF16)
            for half in range(2):
                qh[half, n] = query[:, half * pair:(half + 1) * pair]
            q_copy(n).start()

    low = lax.broadcasted_iota(jnp.int32, (1, pair), 1) < size

    def split_queries():
        for j in range(CHUNKS):
            q_copy(j).wait_recv()
        for side in range(2):
            for j in range(CHUNKS):
                piece = qh[y, j] if side == 0 else qr[j]
                at = side * rows + j * rp
                zero = jnp.zeros_like(piece)
                qm[0, at:at + rp, :] = jnp.where(low, piece, zero)
                qm[1, at:at + rp, :] = jnp.where(low, zero, piece)

    local = rows // BLOCK
    per_chunk = rp // BLOCK
    q_blocks = [order_ref[(line * 2 + side) * local + i] for side in (y, oy) for i in range(local)]
    key_lane = lax.broadcasted_iota(jnp.int32, (1, 2 * rp), 1) // BLOCK

    def attend(n):
        origin, s = slot_of(n)
        y_copy(s).wait_recv()
        keys = jnp.concatenate([kvh[s, y, 0], kvr[s, 0]], axis=0)
        values = jnp.concatenate([kvh[s, y, 1], kvr[s, 1]], axis=0)
        first = (s - origin * CHUNKS) * per_chunk
        k_blocks = [order_ref[(origin * 2 + side) * local + first + i] for side in (y, oy) for i in range(per_chunk)]
        masks = []
        for qb in q_blocks:
            mask = jnp.zeros((1, 2 * rp), F32)
            for i, kb in enumerate(k_blocks):
                mask = jnp.where(key_lane == i, (adj_ref[qb, kb] > 0).astype(F32), mask)
            masks.append(mask)
        ones = jnp.ones_like(values)
        for h in range(2):
            mine = jnp.where(low, values, ones) if h == 0 else jnp.where(low, ones, values)
            scores = lax.dot_general(qm[h], keys, (((1,), (1,)), ((), ())), preferred_element_type=F32)
            probs = jnp.concatenate(
                [(jnp.exp(scores[i * BLOCK:(i + 1) * BLOCK]) * masks[i]).astype(BF16) for i in range(2 * local)], axis=0
            )
            acc[h] += jnp.dot(probs, mine, preferred_element_type=F32)

    def step(n, carry):
        away = n // CHUNKS + 1

        @pl.when(line - away >= 0)
        def _():
            s = (line - away) * CHUNKS + n % CHUNKS
            z_right(s).wait_recv()
            spread(line - away, s)

        @pl.when(line + away < depth)
        def _():
            s = (line + away) * CHUNKS + n % CHUNKS
            z_left(s).wait_recv()
            spread(line + away, s)

        @pl.when(n < total)
        def _():
            origin, s = slot_of(n)
            x_copy(s, xhead).wait_recv()
            c_copy(s, xhead, 1).start()

        @pl.when(jnp.logical_and(n >= 1, n <= total))
        def _():
            project(n - 1)

        @pl.when(n == lag)
        def _():
            split_queries()

        @pl.when(n >= lag)
        def _():
            attend(n - lag)

        return carry

    lax.fori_loop(0, total + lag, step, 0)

    def finish(at):
        first, second = acc[0, at:at + rp, :], acc[1, at:at + rp, :]
        weight = pltpu.roll(jnp.where(low, second, first), size, 1)
        return (jnp.where(low, first, second) / weight).astype(BF16)

    def a_copy(r):
        return remote(asend.at[r], abuf.at[y, r], as_.at[r], ar.at[r], at_y)

    for r in range(CHUNKS):
        asend[r] = finish(rows + r * rp)
        a_copy(r).start()
    for r in range(CHUNKS):
        abuf[y, r] = finish(r * rp)
    for copy in loads[3:]:
        copy.wait()

    def c_out(r, which):
        return remote(csend.at[r, which], crecv.at[r, which], ocs.at[r, which], ocr.at[r, which], at_c)

    x_outs = []
    for r in range(CHUNKS):
        a_copy(r).wait_recv()
        feats = jnp.concatenate([abuf[0, r], abuf[1, r]], axis=1)
        csend[r, 0] = jnp.dot(feats, wo[dhead], preferred_element_type=F32).astype(BF16)
        c_out(r, 0).start()
        part[r, 0] = jnp.dot(feats, wo[xhead], preferred_element_type=F32)
        csend[r, 1] = jnp.dot(feats, wo[chead], preferred_element_type=F32).astype(BF16)
        c_out(r, 1).start()
        part[r, 1] = jnp.dot(feats, wo[head], preferred_element_type=F32)
    for r in range(CHUNKS):
        c_out(r, 0).wait_recv()
        xsend[r] = (part[r, 0] + crecv[r, 0].astype(F32)).astype(BF16)
        x_out = remote(xsend.at[r], xrecv.at[r], oxs.at[r], oxr.at[r], at_x)
        x_out.start()
        x_outs.append(x_out)
    for r in range(CHUNKS):
        c_out(r, 1).wait_recv()
        x_outs[r].wait_recv()
        whole = part[r, 1] + crecv[r, 1].astype(F32) + xrecv[r].astype(F32)
        out_ref[r * rp:(r + 1) * rp, :] = whole.astype(BF16)

    def drain(n, carry):
        origin, s = slot_of(n)

        @pl.when(jnp.logical_and(has_right, origin <= line))
        def _():
            z_right(s).wait_send()

        @pl.when(jnp.logical_and(has_left, origin >= line))
        def _():
            z_left(s).wait_send()

        x_copy(s, head).wait_send()
        c_copy(s, head, 0).wait_send()
        c_copy(s, xhead, 1).wait_send()
        y_copy(s).wait_send()
        return carry

    lax.fori_loop(0, total, drain, 0)
    for j in range(CHUNKS):
        q_copy(j).wait_send()
        c_out(j, 0).wait_send()
        c_out(j, 1).wait_send()
        x_outs[j].wait_send()
        a_copy(j).wait_send()


def shards(depth, tokens, gain, w_query, w_key, w_value, w_out, temper, adjacency, order):
    rows, cols = tokens.shape
    features, width = w_query.shape
    count = features // cols
    pair = width // 2
    rp = rows // CHUNKS
    total = depth * CHUNKS
    dma = pltpu.SemaphoreType.DMA
    smem = pl.BlockSpec(memory_space=pltpu.SMEM)
    vmem = pl.BlockSpec(memory_space=pltpu.VMEM)
    hbm = pl.BlockSpec(memory_space=pl.ANY)
    return pl.pallas_call(
        functools.partial(kernel, depth),
        out_shape=jax.ShapeDtypeStruct((rows, cols), BF16),
        in_specs=[smem, smem, smem, vmem, hbm, hbm, hbm, hbm, hbm],
        out_specs=vmem,
        scratch_shapes=[
            pltpu.VMEM((total, count, rp, cols), BF16),
            pltpu.VMEM((features, width), BF16),
            pltpu.VMEM((features, width), BF16),
            pltpu.VMEM((features, width), BF16),
            pltpu.VMEM((count, width, cols), BF16),
            pltpu.VMEM((width, width), BF16),
            pltpu.VMEM((total, 2, 2, rp, pair), BF16),
            pltpu.VMEM((total, 2, rp, pair), BF16),
            pltpu.VMEM((2, CHUNKS, rp, pair), BF16),
            pltpu.VMEM((CHUNKS, rp, pair), BF16),
            pltpu.VMEM((2, 2 * rows, pair), BF16),
            pltpu.VMEM((2, 2 * rows, pair), F32),
            pltpu.VMEM((CHUNKS, rp, pair), BF16),
            pltpu.VMEM((2, CHUNKS, rp, pair), BF16),
            pltpu.VMEM((CHUNKS, 2, rp, cols), F32),
            pltpu.VMEM((CHUNKS, 2, rp, cols), BF16),
            pltpu.VMEM((CHUNKS, 2, rp, cols), BF16),
            pltpu.VMEM((CHUNKS, rp, cols), BF16),
            pltpu.VMEM((CHUNKS, rp, cols), BF16),
            dma((3 + count,)),
            dma((CHUNKS,)),
            dma((2, total)),
            dma((total,)),
            dma((total,)),
            dma((total,)),
            dma((total, 2)),
            dma((total, 2)),
            dma((total,)),
            dma((total,)),
            dma((CHUNKS,)),
            dma((CHUNKS,)),
            dma((CHUNKS,)),
            dma((CHUNKS,)),
            dma((CHUNKS, 2)),
            dma((CHUNKS, 2)),
            dma((CHUNKS,)),
            dma((CHUNKS,)),
        ],
        compiler_params=pltpu.CompilerParams(
            collective_id=0, has_side_effects=True, vmem_limit_bytes=56 * 1024 * 1024
        ),
    )(order, adjacency, temper, gain.reshape(1, features), tokens, w_query, w_key, w_value, w_out)


def solution(mesh):
    in_specs = (
        P("ctx", "head"),
        P(),
        P(None, "head"),
        P(None, "head"),
        P(None, "head"),
        P("head", None),
        P("head"),
        P(),
        P(),
    )
    out_specs = P("ctx", "head")
    body = functools.partial(shards, mesh.shape["ctx"] // 2)
    return jax.shard_map(body, mesh=mesh, in_specs=in_specs, out_specs=out_specs, check_vma=False)
```

```python
import functools

import jax
import jax.numpy as jnp
from jax import lax
from jax.experimental import pallas as pl
from jax.experimental.pallas import tpu as pltpu
from jax.sharding import PartitionSpec as P

BLOCK = 128
CHUNKS = 1
TAIL = 2
EPS = 1e-06
LOG2E = 1.4426950408889634
MESH = pl.DeviceIdType.MESH
F32 = jnp.float32
BF16 = jnp.bfloat16


def visit(line, depth, n):
    far = depth - 1 - line
    near = jnp.minimum(line, far) * CHUNKS
    p = n - CHUNKS
    paired = p < 2 * near
    t = jnp.where(paired, p // 2, p - near)
    to_left = jnp.where(paired, p % 2 == 0, line > far)
    away = t // CHUNKS + 1
    origin = jnp.where(n < CHUNKS, line, jnp.where(to_left, line - away, line + away))
    return origin, jnp.where(n < CHUNKS, n, t % CHUNKS)


def kernel(
    depth,
    order_ref, adj_ref, temper_ref, gain_ref, tokens_ref, wq_hbm, wk_hbm, wv_hbm, wo_hbm,
    out_ref,
    tok, wq, wk, wv, wo, mean_mat, kvh, kvr, qh, qr, qm, acc, asend, abuf, part, csend, crecv, xsend, xrecv,
    w_sem, t_sem, zs, zr, xs, xr, cs, cr, ys, yr, qs, qrs, as_, ar, ocs, ocr, oxs, oxr,
):
    ctx, head = lax.axis_index("ctx"), lax.axis_index("head")
    line, y = ctx // 2, ctx % 2
    x, c = head // 2, head % 2
    oy, ox, oc = 1 - y, 1 - x, 1 - c
    rows, cols = tokens_ref.shape
    heads = temper_ref.shape[0]
    width = wq.shape[1]
    size = width // heads
    pair = width // 2
    rp = rows // CHUNKS
    total = depth * CHUNKS
    features = wq.shape[0]
    lag = CHUNKS + 1
    has_left, has_right = line > 0, line < depth - 1
    at_left, at_right = (ctx - 2, head), (ctx + 2, head)
    at_y = (line * 2 + oy, head)
    at_x = (ctx, ox * 2 + c)
    at_c = (ctx, x * 2 + oc)
    xhead = ox * 2 + c
    chead = x * 2 + oc
    dhead = ox * 2 + oc

    def remote(src, dst, send, recv, where):
        return pltpu.make_async_remote_copy(
            src_ref=src, dst_ref=dst, send_sem=send, recv_sem=recv, device_id=where, device_id_type=MESH
        )

    loads = [
        pltpu.make_async_copy(wk_hbm, wk, w_sem.at[0]),
        pltpu.make_async_copy(wv_hbm, wv, w_sem.at[1]),
        pltpu.make_async_copy(wq_hbm, wq, w_sem.at[2]),
    ]
    count = wo.shape[0]
    for h in range(count):
        loads.append(pltpu.make_async_copy(wo_hbm.at[:, pl.ds(h * cols, cols)], wo.at[h], w_sem.at[3 + h]))
    own = [
        pltpu.make_async_copy(tokens_ref.at[pl.ds(j * rp, rp), :], tok.at[line * CHUNKS + j, head], t_sem.at[j])
        for j in range(CHUNKS)
    ]
    for copy in own + loads:
        copy.start()

    barrier = pltpu.get_barrier_semaphore()
    for where in (at_y, at_x, at_c):
        pl.semaphore_signal(barrier, inc=1, device_id=where, device_id_type=MESH)

    @pl.when(has_left)
    def _():
        pl.semaphore_signal(barrier, inc=1, device_id=at_left, device_id_type=MESH)

    @pl.when(has_right)
    def _():
        pl.semaphore_signal(barrier, inc=1, device_id=at_right, device_id_type=MESH)

    row_id = lax.broadcasted_iota(jnp.int32, (width, width), 0) // size
    col_id = lax.broadcasted_iota(jnp.int32, (width, width), 1) // size
    mean_mat[...] = jnp.where(row_id == col_id, 1.0 / size, 0.0).astype(BF16)
    acc[...] = jnp.zeros_like(acc)
    pl.semaphore_wait(barrier, 3 + has_left.astype(jnp.int32) + has_right.astype(jnp.int32))

    def slot_of(n):
        origin, j = visit(line, depth, n)
        return origin, origin * CHUNKS + j

    def z_right(s):
        return remote(tok.at[s, head], tok.at[s, head], zs.at[1, s], zr.at[s], at_right)

    def z_left(s):
        return remote(tok.at[s, head], tok.at[s, head], zs.at[0, s], zr.at[s], at_left)

    def x_copy(s, h):
        return remote(tok.at[s, h], tok.at[s, h], xs.at[s], xr.at[s], at_x)

    def c_copy(s, h, which):
        return remote(tok.at[s, h], tok.at[s, h], cs.at[s, which], cr.at[s, which], at_c)

    def y_copy(s):
        return remote(kvh.at[s, oy], kvr.at[s], ys.at[s], yr.at[s], at_y)

    def q_copy(j):
        return remote(qh.at[oy, j], qr.at[j], qs.at[j], qrs.at[j], at_y)

    def spread(origin, s):
        @pl.when(jnp.logical_and(has_right, origin <= line))
        def _():
            z_right(s).start()

        @pl.when(jnp.logical_and(has_left, origin >= line))
        def _():
            z_left(s).start()

        x_copy(s, head).start()
        c_copy(s, head, 0).start()

    for j in range(CHUNKS):
        own[j].wait()
        spread(line, line * CHUNKS + j)
    for copy in loads[:3]:
        copy.wait()

    def unit(values):
        mean = jnp.dot((values * values).astype(BF16), mean_mat[...], preferred_element_type=F32)
        return values * lax.rsqrt(mean + EPS)

    lane_w = lax.broadcasted_iota(jnp.int32, (1, width), 1) // size
    scale = jnp.zeros((1, width), F32)
    for h in range(heads):
        scale = jnp.where(lane_w == h, temper_ref[h] * (LOG2E / size), scale)

    def project(n):
        origin, s = slot_of(n)
        c_copy(s, chead, 0).wait_recv()
        c_copy(s, dhead, 1).wait_recv()
        parts = [tok[s, h].astype(F32) for h in range(count)]
        squares = parts[0] * parts[0]
        for p in parts[1:]:
            squares = squares + p * p
        inv = lax.rsqrt(jnp.sum(squares, axis=-1, keepdims=True) * (1.0 / features) + EPS)
        normed = jnp.concatenate(
            [(parts[h] * inv * gain_ref[:, h * cols:(h + 1) * cols]).astype(BF16) for h in range(count)], axis=1
        )
        keys = unit(jnp.dot(normed, wk[...], preferred_element_type=F32)).astype(BF16)
        values = jnp.dot(normed, wv[...], preferred_element_type=F32).astype(BF16)
        for half in range(2):
            kvh[s, half, 0] = keys[:, half * pair:(half + 1) * pair]
            kvh[s, half, 1] = values[:, half * pair:(half + 1) * pair]
        y_copy(s).start()

        @pl.when(n < CHUNKS)
        def _():
            query = unit(jnp.dot(normed, wq[...], preferred_element_type=F32))
            query = (query * scale).astype(BF16)
            for half in range(2):
                qh[half, n] = query[:, half * pair:(half + 1) * pair]
            q_copy(n).start()

    low = lax.broadcasted_iota(jnp.int32, (1, pair), 1) < size

    def split_queries():
        for j in range(CHUNKS):
            q_copy(j).wait_recv()
        for side in range(2):
            for j in range(CHUNKS):
                piece = qh[y, j] if side == 0 else qr[j]
                at = side * rows + j * rp
                zero = jnp.zeros_like(piece)
                qm[0, at:at + rp, :] = jnp.where(low, piece, zero)
                qm[1, at:at + rp, :] = jnp.where(low, zero, piece)

    local = rows // BLOCK
    per_chunk = rp // BLOCK
    q_blocks = [order_ref[(line * 2 + side) * local + i] for side in (y, oy) for i in range(local)]
    key_lane = lax.broadcasted_iota(jnp.int32, (1, 2 * rp), 1) // BLOCK

    def attend(n):
        origin, s = slot_of(n)
        y_copy(s).wait_recv()
        keys = jnp.concatenate([kvh[s, y, 0], kvr[s, 0]], axis=0)
        values = jnp.concatenate([kvh[s, y, 1], kvr[s, 1]], axis=0)
        first = (s - origin * CHUNKS) * per_chunk
        k_blocks = [order_ref[(origin * 2 + side) * local + first + i] for side in (y, oy) for i in range(per_chunk)]
        masks = []
        for qb in q_blocks:
            mask = jnp.zeros((1, 2 * rp), F32)
            for i, kb in enumerate(k_blocks):
                mask = jnp.where(key_lane == i, (adj_ref[qb, kb] > 0).astype(F32), mask)
            masks.append(mask)
        ones = jnp.ones_like(values)
        for h in range(2):
            mine = jnp.where(low, values, ones) if h == 0 else jnp.where(low, ones, values)
            scores = lax.dot_general(qm[h], keys, (((1,), (1,)), ((), ())), preferred_element_type=F32)
            probs = jnp.concatenate(
                [(jnp.exp2(scores[i * BLOCK:(i + 1) * BLOCK]) * masks[i]).astype(BF16) for i in range(2 * local)], axis=0
            )
            acc[h] += jnp.dot(probs, mine, preferred_element_type=F32)

    def step(n, carry):
        away = n // CHUNKS + 1

        @pl.when(line - away >= 0)
        def _():
            s = (line - away) * CHUNKS + n % CHUNKS
            z_right(s).wait_recv()
            spread(line - away, s)

        @pl.when(line + away < depth)
        def _():
            s = (line + away) * CHUNKS + n % CHUNKS
            z_left(s).wait_recv()
            spread(line + away, s)

        @pl.when(n < total)
        def _():
            origin, s = slot_of(n)
            x_copy(s, xhead).wait_recv()
            c_copy(s, xhead, 1).start()

        @pl.when(jnp.logical_and(n >= 1, n <= total))
        def _():
            project(n - 1)

        @pl.when(n == lag)
        def _():
            split_queries()

        @pl.when(n >= lag)
        def _():
            attend(n - lag)

        return carry

    lax.fori_loop(0, total + lag, step, 0)

    tp = rows // TAIL

    def finish(at):
        first, second = acc[0, at:at + tp, :], acc[1, at:at + tp, :]
        weight = pltpu.roll(jnp.where(low, second, first), size, 1)
        return (jnp.where(low, first, second) / weight).astype(BF16)

    def a_copy(r):
        return remote(asend.at[r], abuf.at[y, r], as_.at[r], ar.at[r], at_y)

    for r in range(TAIL):
        asend[r] = finish(rows + r * tp)
        a_copy(r).start()
    for r in range(TAIL):
        abuf[y, r] = finish(r * tp)
    for copy in loads[3:]:
        copy.wait()

    def c_out(r, which):
        return remote(csend.at[r, which], crecv.at[r, which], ocs.at[r, which], ocr.at[r, which], at_c)

    x_outs = []
    for r in range(TAIL):
        a_copy(r).wait_recv()
        feats = jnp.concatenate([abuf[0, r], abuf[1, r]], axis=1)
        csend[r, 0] = jnp.dot(feats, wo[dhead], preferred_element_type=F32).astype(BF16)
        c_out(r, 0).start()
        part[r, 0] = jnp.dot(feats, wo[xhead], preferred_element_type=F32)
        csend[r, 1] = jnp.dot(feats, wo[chead], preferred_element_type=F32).astype(BF16)
        c_out(r, 1).start()
        part[r, 1] = jnp.dot(feats, wo[head], preferred_element_type=F32)
    for r in range(TAIL):
        c_out(r, 0).wait_recv()
        xsend[r] = (part[r, 0] + crecv[r, 0].astype(F32)).astype(BF16)
        x_out = remote(xsend.at[r], xrecv.at[r], oxs.at[r], oxr.at[r], at_x)
        x_out.start()
        x_outs.append(x_out)
    for r in range(TAIL):
        c_out(r, 1).wait_recv()
        x_outs[r].wait_recv()
        whole = part[r, 1] + crecv[r, 1].astype(F32) + xrecv[r].astype(F32)
        out_ref[r * tp:(r + 1) * tp, :] = whole.astype(BF16)

    def drain(n, carry):
        origin, s = slot_of(n)

        @pl.when(jnp.logical_and(has_right, origin <= line))
        def _():
            z_right(s).wait_send()

        @pl.when(jnp.logical_and(has_left, origin >= line))
        def _():
            z_left(s).wait_send()

        x_copy(s, head).wait_send()
        c_copy(s, head, 0).wait_send()
        c_copy(s, xhead, 1).wait_send()
        y_copy(s).wait_send()
        return carry

    lax.fori_loop(0, total, drain, 0)
    for j in range(CHUNKS):
        q_copy(j).wait_send()
    for j in range(TAIL):
        c_out(j, 0).wait_send()
        c_out(j, 1).wait_send()
        x_outs[j].wait_send()
        a_copy(j).wait_send()


def shards(depth, tokens, gain, w_query, w_key, w_value, w_out, temper, adjacency, order):
    rows, cols = tokens.shape
    features, width = w_query.shape
    count = features // cols
    pair = width // 2
    rp = rows // CHUNKS
    tp = rows // TAIL
    total = depth * CHUNKS
    dma = pltpu.SemaphoreType.DMA
    smem = pl.BlockSpec(memory_space=pltpu.SMEM)
    vmem = pl.BlockSpec(memory_space=pltpu.VMEM)
    hbm = pl.BlockSpec(memory_space=pl.ANY)
    return pl.pallas_call(
        functools.partial(kernel, depth),
        out_shape=jax.ShapeDtypeStruct((rows, cols), BF16),
        in_specs=[smem, smem, smem, vmem, hbm, hbm, hbm, hbm, hbm],
        out_specs=vmem,
        scratch_shapes=[
            pltpu.VMEM((total, count, rp, cols), BF16),
            pltpu.VMEM((features, width), BF16),
            pltpu.VMEM((features, width), BF16),
            pltpu.VMEM((features, width), BF16),
            pltpu.VMEM((count, width, cols), BF16),
            pltpu.VMEM((width, width), BF16),
            pltpu.VMEM((total, 2, 2, rp, pair), BF16),
            pltpu.VMEM((total, 2, rp, pair), BF16),
            pltpu.VMEM((2, CHUNKS, rp, pair), BF16),
            pltpu.VMEM((CHUNKS, rp, pair), BF16),
            pltpu.VMEM((2, 2 * rows, pair), BF16),
            pltpu.VMEM((2, 2 * rows, pair), F32),
            pltpu.VMEM((TAIL, tp, pair), BF16),
            pltpu.VMEM((2, TAIL, tp, pair), BF16),
            pltpu.VMEM((TAIL, 2, tp, cols), F32),
            pltpu.VMEM((TAIL, 2, tp, cols), BF16),
            pltpu.VMEM((TAIL, 2, tp, cols), BF16),
            pltpu.VMEM((TAIL, tp, cols), BF16),
            pltpu.VMEM((TAIL, tp, cols), BF16),
            dma((3 + count,)),
            dma((CHUNKS,)),
            dma((2, total)),
            dma((total,)),
            dma((total,)),
            dma((total,)),
            dma((total, 2)),
            dma((total, 2)),
            dma((total,)),
            dma((total,)),
            dma((CHUNKS,)),
            dma((CHUNKS,)),
            dma((TAIL,)),
            dma((TAIL,)),
            dma((TAIL, 2)),
            dma((TAIL, 2)),
            dma((TAIL,)),
            dma((TAIL,)),
        ],
        compiler_params=pltpu.CompilerParams(
            collective_id=0, has_side_effects=True, vmem_limit_bytes=56 * 1024 * 1024
        ),
    )(order, adjacency, temper, gain.reshape(1, features), tokens, w_query, w_key, w_value, w_out)


def solution(mesh):
    in_specs = (
        P("ctx", "head"),
        P(),
        P(None, "head"),
        P(None, "head"),
        P(None, "head"),
        P("head", None),
        P("head"),
        P(),
        P(),
    )
    out_specs = P("ctx", "head")
    body = functools.partial(shards, mesh.shape["ctx"] // 2)
    return jax.shard_map(body, mesh=mesh, in_specs=in_specs, out_specs=out_specs, check_vma=False)
```

```python
import functools

import jax
import jax.numpy as jnp
from jax import lax
from jax.experimental import pallas as pl
from jax.experimental.pallas import tpu as pltpu
from jax.sharding import PartitionSpec as P

BLOCK = 128
CHUNKS = 2
TAIL = 2
EPS = 1e-06
LOG2E = 1.4426950408889634
MESH = pl.DeviceIdType.MESH
F32 = jnp.float32
BF16 = jnp.bfloat16


def visit(line, depth, n):
    far = depth - 1 - line
    near = jnp.minimum(line, far) * CHUNKS
    p = n - CHUNKS
    paired = p < 2 * near
    t = jnp.where(paired, p // 2, p - near)
    to_left = jnp.where(paired, p % 2 == 0, line > far)
    away = t // CHUNKS + 1
    origin = jnp.where(n < CHUNKS, line, jnp.where(to_left, line - away, line + away))
    return origin, jnp.where(n < CHUNKS, n, t % CHUNKS)


def kernel(
    depth,
    order_ref, adj_ref, temper_ref, gain_ref, tokens_ref, wq_hbm, wk_hbm, wv_hbm, wo_hbm,
    all_ref, wall_ref,
    tok, wq, wk, wv, mean_mat, kvh, kvr, qh, qr, qm, acc, asend, abuf, xbuf,
    w_sem, t_sem, zs, zr, xs, xr, cs, cr, ys, yr, qs, qrs, as_, ar, axs, axr, acs, acr, al, ws, wr, wl,
):
    ctx, head = lax.axis_index("ctx"), lax.axis_index("head")
    line, y = ctx // 2, ctx % 2
    x, c = head // 2, head % 2
    oy, ox, oc = 1 - y, 1 - x, 1 - c
    rows, cols = tokens_ref.shape
    heads = temper_ref.shape[0]
    width = wq.shape[1]
    size = width // heads
    pair = width // 2
    rp = rows // CHUNKS
    total = depth * CHUNKS
    features = wq.shape[0]
    lag = CHUNKS + 1
    has_left, has_right = line > 0, line < depth - 1
    at_left, at_right = (ctx - 2, head), (ctx + 2, head)
    at_y = (line * 2 + oy, head)
    at_x = (ctx, ox * 2 + c)
    at_c = (ctx, x * 2 + oc)
    xhead = ox * 2 + c
    chead = x * 2 + oc
    dhead = ox * 2 + oc
    at_d = (ctx, dhead)

    def remote(src, dst, send, recv, where):
        return pltpu.make_async_remote_copy(
            src_ref=src, dst_ref=dst, send_sem=send, recv_sem=recv, device_id=where, device_id_type=MESH
        )

    loads = [
        pltpu.make_async_copy(wk_hbm, wk, w_sem.at[0]),
        pltpu.make_async_copy(wv_hbm, wv, w_sem.at[1]),
        pltpu.make_async_copy(wq_hbm, wq, w_sem.at[2]),
    ]
    count = features // cols
    own = [
        pltpu.make_async_copy(tokens_ref.at[pl.ds(j * rp, rp), :], tok.at[line * CHUNKS + j, head], t_sem.at[j])
        for j in range(CHUNKS)
    ]
    for copy in own + loads:
        copy.start()

    barrier = pltpu.get_barrier_semaphore()
    for where in (at_y, at_x, at_c, at_d):
        pl.semaphore_signal(barrier, inc=1, device_id=where, device_id_type=MESH)

    @pl.when(has_left)
    def _():
        pl.semaphore_signal(barrier, inc=1, device_id=at_left, device_id_type=MESH)

    @pl.when(has_right)
    def _():
        pl.semaphore_signal(barrier, inc=1, device_id=at_right, device_id_type=MESH)

    row_id = lax.broadcasted_iota(jnp.int32, (width, width), 0) // size
    col_id = lax.broadcasted_iota(jnp.int32, (width, width), 1) // size
    mean_mat[...] = jnp.where(row_id == col_id, 1.0 / size, 0.0).astype(BF16)
    acc[...] = jnp.zeros_like(acc)
    pl.semaphore_wait(barrier, 4 + has_left.astype(jnp.int32) + has_right.astype(jnp.int32))

    def slot_of(n):
        origin, j = visit(line, depth, n)
        return origin, origin * CHUNKS + j

    def z_right(s):
        return remote(tok.at[s, head], tok.at[s, head], zs.at[1, s], zr.at[s], at_right)

    def z_left(s):
        return remote(tok.at[s, head], tok.at[s, head], zs.at[0, s], zr.at[s], at_left)

    def x_copy(s, h):
        return remote(tok.at[s, h], tok.at[s, h], xs.at[s], xr.at[s], at_x)

    def c_copy(s, h, which):
        return remote(tok.at[s, h], tok.at[s, h], cs.at[s, which], cr.at[s, which], at_c)

    def y_copy(s):
        return remote(kvh.at[s, oy], kvr.at[s], ys.at[s], yr.at[s], at_y)

    def q_copy(j):
        return remote(qh.at[oy, j], qr.at[j], qs.at[j], qrs.at[j], at_y)

    def spread(origin, s):
        @pl.when(jnp.logical_and(has_right, origin <= line))
        def _():
            z_right(s).start()

        @pl.when(jnp.logical_and(has_left, origin >= line))
        def _():
            z_left(s).start()

        x_copy(s, head).start()
        c_copy(s, head, 0).start()

    for j in range(CHUNKS):
        own[j].wait()
        spread(line, line * CHUNKS + j)
    for copy in loads:
        copy.wait()

    def unit(values):
        mean = jnp.dot((values * values).astype(BF16), mean_mat[...], preferred_element_type=F32)
        return values * lax.rsqrt(mean + EPS)

    lane_w = lax.broadcasted_iota(jnp.int32, (1, width), 1) // size
    scale = jnp.zeros((1, width), F32)
    for h in range(heads):
        scale = jnp.where(lane_w == h, temper_ref[h] * (LOG2E / size), scale)

    def project(n):
        origin, s = slot_of(n)
        c_copy(s, chead, 0).wait_recv()
        c_copy(s, dhead, 1).wait_recv()
        parts = [tok[s, h].astype(F32) for h in range(count)]
        squares = parts[0] * parts[0]
        for p in parts[1:]:
            squares = squares + p * p
        inv = lax.rsqrt(jnp.sum(squares, axis=-1, keepdims=True) * (1.0 / features) + EPS)
        normed = jnp.concatenate(
            [(parts[h] * inv * gain_ref[:, h * cols:(h + 1) * cols]).astype(BF16) for h in range(count)], axis=1
        )
        keys = unit(jnp.dot(normed, wk[...], preferred_element_type=F32)).astype(BF16)
        values = jnp.dot(normed, wv[...], preferred_element_type=F32).astype(BF16)
        for half in range(2):
            kvh[s, half, 0] = keys[:, half * pair:(half + 1) * pair]
            kvh[s, half, 1] = values[:, half * pair:(half + 1) * pair]
        y_copy(s).start()

        @pl.when(n < CHUNKS)
        def _():
            query = unit(jnp.dot(normed, wq[...], preferred_element_type=F32))
            query = (query * scale).astype(BF16)
            for half in range(2):
                qh[half, n] = query[:, half * pair:(half + 1) * pair]
            q_copy(n).start()

    low = lax.broadcasted_iota(jnp.int32, (1, pair), 1) < size

    def split_queries():
        for j in range(CHUNKS):
            q_copy(j).wait_recv()
        for side in range(2):
            for j in range(CHUNKS):
                piece = qh[y, j] if side == 0 else qr[j]
                at = side * rows + j * rp
                zero = jnp.zeros_like(piece)
                qm[0, at:at + rp, :] = jnp.where(low, piece, zero)
                qm[1, at:at + rp, :] = jnp.where(low, zero, piece)

    local = rows // BLOCK
    per_chunk = rp // BLOCK
    q_blocks = [order_ref[(line * 2 + side) * local + i] for side in (y, oy) for i in range(local)]
    key_lane = lax.broadcasted_iota(jnp.int32, (1, 2 * rp), 1) // BLOCK

    def attend(n):
        origin, s = slot_of(n)
        y_copy(s).wait_recv()
        keys = jnp.concatenate([kvh[s, y, 0], kvr[s, 0]], axis=0)
        values = jnp.concatenate([kvh[s, y, 1], kvr[s, 1]], axis=0)
        first = (s - origin * CHUNKS) * per_chunk
        k_blocks = [order_ref[(origin * 2 + side) * local + first + i] for side in (y, oy) for i in range(per_chunk)]
        masks = []
        for qb in q_blocks:
            mask = jnp.zeros((1, 2 * rp), F32)
            for i, kb in enumerate(k_blocks):
                mask = jnp.where(key_lane == i, (adj_ref[qb, kb] > 0).astype(F32), mask)
            masks.append(mask)
        ones = jnp.ones_like(values)
        for h in range(2):
            mine = jnp.where(low, values, ones) if h == 0 else jnp.where(low, ones, values)
            scores = lax.dot_general(qm[h], keys, (((1,), (1,)), ((), ())), preferred_element_type=F32)
            probs = jnp.concatenate(
                [(jnp.exp2(scores[i * BLOCK:(i + 1) * BLOCK]) * masks[i]).astype(BF16) for i in range(2 * local)], axis=0
            )
            acc[h] += jnp.dot(probs, mine, preferred_element_type=F32)

    def w_columns(h):
        return wo_hbm.at[:, pl.ds(pl.multiple_of(h * cols, cols), cols)]

    def w_rows(h):
        return wall_ref.at[pl.ds(pl.multiple_of(h * width, width), width), :]

    def w_copy(which):
        h, where = ((xhead, at_x), (dhead, at_d), (chead, at_c))[which]
        return remote(w_columns(h), w_rows(head), ws.at[which], wr.at[which], where)

    def w_own():
        return pltpu.make_async_copy(w_columns(head), w_rows(head), wl)

    def step(n, carry):
        away = n // CHUNKS + 1

        @pl.when(line - away >= 0)
        def _():
            s = (line - away) * CHUNKS + n % CHUNKS
            z_right(s).wait_recv()
            spread(line - away, s)

        @pl.when(line + away < depth)
        def _():
            s = (line + away) * CHUNKS + n % CHUNKS
            z_left(s).wait_recv()
            spread(line + away, s)

        @pl.when(n < total)
        def _():
            origin, s = slot_of(n)
            x_copy(s, xhead).wait_recv()
            c_copy(s, xhead, 1).start()

        @pl.when(n == total - 1)
        def _():
            for which in range(3):
                w_copy(which).start()
            w_own().start()

        @pl.when(jnp.logical_and(n >= 1, n <= total))
        def _():
            project(n - 1)

        @pl.when(n == lag)
        def _():
            split_queries()

        @pl.when(n >= lag)
        def _():
            attend(n - lag)

        return carry

    lax.fori_loop(0, total + lag, step, 0)

    tp = rows // TAIL

    def finish(at):
        first, second = acc[0, at:at + tp, :], acc[1, at:at + tp, :]
        weight = pltpu.roll(jnp.where(low, second, first), size, 1)
        return (jnp.where(low, first, second) / weight).astype(BF16)

    def block(h, half, r):
        at = pl.multiple_of((h * 2 + half) * pair, pair)
        return all_ref.at[pl.ds(r * tp, tp), pl.ds(at, pair)]

    def a_copy(r):
        return remote(asend.at[r], abuf.at[y, r], as_.at[r], ar.at[r], at_y)

    def ax_copy(half, r, k):
        return remote(abuf.at[half, r], xbuf.at[half, r], axs.at[k, r], axr.at[k, r], at_x)

    def ac_copy(src, h, half, r, k):
        return remote(src.at[half, r], block(h, half, r), acs.at[k, r], acr.at[k, r], at_c)

    def keep(src, h, half, r, k):
        return pltpu.make_async_copy(src.at[half, r], block(h, half, r), al.at[k, r])

    for r in range(TAIL):
        asend[r] = finish(rows + r * tp)
        a_copy(r).start()
    for r in range(TAIL):
        abuf[y, r] = finish(r * tp)
        ax_copy(y, r, 0).start()
    for r in range(TAIL):
        ac_copy(abuf, head, y, r, 0).start()
        keep(abuf, head, y, r, 0).start()
    for r in range(TAIL):
        a_copy(r).wait_recv()
        ax_copy(oy, r, 1).start()
        ac_copy(abuf, head, oy, r, 1).start()
        keep(abuf, head, oy, r, 1).start()
    for k, half in ((0, y), (1, oy)):
        for r in range(TAIL):
            ax_copy(half, r, k).wait_recv()
            ac_copy(xbuf, xhead, half, r, 2 + k).start()
            keep(xbuf, xhead, half, r, 2 + k).start()

    def drain(n, carry):
        origin, s = slot_of(n)

        @pl.when(jnp.logical_and(has_right, origin <= line))
        def _():
            z_right(s).wait_send()

        @pl.when(jnp.logical_and(has_left, origin >= line))
        def _():
            z_left(s).wait_send()

        x_copy(s, head).wait_send()
        c_copy(s, head, 0).wait_send()
        c_copy(s, xhead, 1).wait_send()
        y_copy(s).wait_send()
        return carry

    lax.fori_loop(0, total, drain, 0)
    for j in range(CHUNKS):
        q_copy(j).wait_send()
    for which in range(3):
        w_copy(which).wait()
    w_own().wait()
    for r in range(TAIL):
        a_copy(r).wait_send()
        for k, half in ((0, y), (1, oy)):
            ax_copy(half, r, k).wait_send()
            for base, src, h in ((0, abuf, head), (2, xbuf, xhead)):
                ac_copy(src, h, half, r, base + k).wait()
                keep(src, h, half, r, base + k).wait()


def shards(depth, tokens, gain, w_query, w_key, w_value, w_out, temper, adjacency, order):
    rows, cols = tokens.shape
    features, width = w_query.shape
    count = features // cols
    pair = width // 2
    rp = rows // CHUNKS
    tp = rows // TAIL
    total = depth * CHUNKS
    dma = pltpu.SemaphoreType.DMA
    smem = pl.BlockSpec(memory_space=pltpu.SMEM)
    vmem = pl.BlockSpec(memory_space=pltpu.VMEM)
    hbm = pl.BlockSpec(memory_space=pl.ANY)
    attended, weights = pl.pallas_call(
        functools.partial(kernel, depth),
        out_shape=(
            jax.ShapeDtypeStruct((rows, count * width), BF16),
            jax.ShapeDtypeStruct((count * width, cols), BF16),
        ),
        in_specs=[smem, smem, smem, vmem, hbm, hbm, hbm, hbm, hbm],
        out_specs=(hbm, hbm),
        scratch_shapes=[
            pltpu.VMEM((total, count, rp, cols), BF16),
            pltpu.VMEM((features, width), BF16),
            pltpu.VMEM((features, width), BF16),
            pltpu.VMEM((features, width), BF16),
            pltpu.VMEM((width, width), BF16),
            pltpu.VMEM((total, 2, 2, rp, pair), BF16),
            pltpu.VMEM((total, 2, rp, pair), BF16),
            pltpu.VMEM((2, CHUNKS, rp, pair), BF16),
            pltpu.VMEM((CHUNKS, rp, pair), BF16),
            pltpu.VMEM((2, 2 * rows, pair), BF16),
            pltpu.VMEM((2, 2 * rows, pair), F32),
            pltpu.VMEM((TAIL, tp, pair), BF16),
            pltpu.VMEM((2, TAIL, tp, pair), BF16),
            pltpu.VMEM((2, TAIL, tp, pair), BF16),
            dma((3,)),
            dma((CHUNKS,)),
            dma((2, total)),
            dma((total,)),
            dma((total,)),
            dma((total,)),
            dma((total, 2)),
            dma((total, 2)),
            dma((total,)),
            dma((total,)),
            dma((CHUNKS,)),
            dma((CHUNKS,)),
            dma((TAIL,)),
            dma((TAIL,)),
            dma((2, TAIL)),
            dma((2, TAIL)),
            dma((4, TAIL)),
            dma((4, TAIL)),
            dma((4, TAIL)),
            dma((3,)),
            dma((3,)),
            dma,
        ],
        compiler_params=pltpu.CompilerParams(
            collective_id=0, has_side_effects=True, vmem_limit_bytes=56 * 1024 * 1024
        ),
    )(order, adjacency, temper, gain.reshape(1, features), tokens, w_query, w_key, w_value, w_out)
    return jnp.dot(attended, weights, preferred_element_type=F32).astype(BF16)


def solution(mesh):
    in_specs = (
        P("ctx", "head"),
        P(),
        P(None, "head"),
        P(None, "head"),
        P(None, "head"),
        P("head", None),
        P("head"),
        P(),
        P(),
    )
    out_specs = P("ctx", "head")
    body = functools.partial(shards, mesh.shape["ctx"] // 2)
    return jax.shard_map(body, mesh=mesh, in_specs=in_specs, out_specs=out_specs, check_vma=False)
```

```python
import functools

import jax
import jax.numpy as jnp
from jax import lax
from jax.experimental import pallas as pl
from jax.experimental.pallas import tpu as pltpu
from jax.sharding import PartitionSpec as P

BLOCK = 128
CHUNKS = 2
TAIL = 2
EPS = 1e-06
LOG2E = 1.4426950408889634
MESH = pl.DeviceIdType.MESH
F32 = jnp.float32
BF16 = jnp.bfloat16


def visit(line, depth, n):
    far = depth - 1 - line
    near = jnp.minimum(line, far) * CHUNKS
    p = n - CHUNKS
    paired = p < 2 * near
    t = jnp.where(paired, p // 2, p - near)
    to_left = jnp.where(paired, p % 2 == 0, line > far)
    away = t // CHUNKS + 1
    origin = jnp.where(n < CHUNKS, line, jnp.where(to_left, line - away, line + away))
    return origin, jnp.where(n < CHUNKS, n, t % CHUNKS)


def kernel(
    depth,
    order_ref, adj_ref, temper_ref, gain_ref, tokens_ref, wq_hbm, wk_hbm, wv_hbm, wo_hbm,
    all_ref, wall_ref,
    tok, wq, wk, wv, mean_mat, kvh, kvr, qh, qr, qm, acc, asend, abuf, xbuf,
    w_sem, t_sem, zs, zr, xs, xr, cs, cr, ys, yr, qs, qrs, as_, ar, axs, axr, acs, acr, al, ws, wr, wl,
):
    ctx, head = lax.axis_index("ctx"), lax.axis_index("head")
    line, y = ctx // 2, ctx % 2
    x, c = head // 2, head % 2
    oy, ox, oc = 1 - y, 1 - x, 1 - c
    rows, cols = tokens_ref.shape
    heads = temper_ref.shape[0]
    width = wq.shape[1]
    size = width // heads
    pair = width // 2
    rp = rows // CHUNKS
    total = depth * CHUNKS
    features = wq.shape[0]
    lag = CHUNKS + 2
    has_left, has_right = line > 0, line < depth - 1
    at_left, at_right = (ctx - 2, head), (ctx + 2, head)
    at_y = (line * 2 + oy, head)
    at_x = (ctx, ox * 2 + c)
    at_xy = (line * 2 + oy, ox * 2 + c)
    at_c = (ctx, x * 2 + oc)
    xhead = ox * 2 + c
    chead = x * 2 + oc
    dhead = ox * 2 + oc
    at_d = (ctx, dhead)

    def remote(src, dst, send, recv, where):
        return pltpu.make_async_remote_copy(
            src_ref=src, dst_ref=dst, send_sem=send, recv_sem=recv, device_id=where, device_id_type=MESH
        )

    loads = [
        pltpu.make_async_copy(wk_hbm, wk, w_sem.at[0]),
        pltpu.make_async_copy(wv_hbm, wv, w_sem.at[1]),
        pltpu.make_async_copy(wq_hbm, wq, w_sem.at[2]),
    ]
    count = features // cols
    own = [
        pltpu.make_async_copy(tokens_ref.at[pl.ds(j * rp, rp), :], tok.at[line * CHUNKS + j, head], t_sem.at[j])
        for j in range(CHUNKS)
    ]
    for copy in own + loads:
        copy.start()

    barrier = pltpu.get_barrier_semaphore()
    for where in (at_y, at_x, at_c, at_d, at_xy):
        pl.semaphore_signal(barrier, inc=1, device_id=where, device_id_type=MESH)

    @pl.when(has_left)
    def _():
        pl.semaphore_signal(barrier, inc=1, device_id=at_left, device_id_type=MESH)

    @pl.when(has_right)
    def _():
        pl.semaphore_signal(barrier, inc=1, device_id=at_right, device_id_type=MESH)

    row_id = lax.broadcasted_iota(jnp.int32, (width, width), 0) // size
    col_id = lax.broadcasted_iota(jnp.int32, (width, width), 1) // size
    mean_mat[...] = jnp.where(row_id == col_id, 1.0 / size, 0.0).astype(BF16)
    acc[...] = jnp.zeros_like(acc)
    pl.semaphore_wait(barrier, 5 + has_left.astype(jnp.int32) + has_right.astype(jnp.int32))

    def slot_of(n):
        origin, j = visit(line, depth, n)
        return origin, origin * CHUNKS + j

    def z_right(s):
        return remote(tok.at[s, head], tok.at[s, head], zs.at[1, s], zr.at[s], at_right)

    def z_left(s):
        return remote(tok.at[s, head], tok.at[s, head], zs.at[0, s], zr.at[s], at_left)

    def x_copy(s, h):
        return remote(tok.at[s, h], tok.at[s, h], xs.at[s], xr.at[s], at_x)

    def c_copy(s, h, which):
        return remote(tok.at[s, h], tok.at[s, h], cs.at[s, which], cr.at[s, which], at_c)

    def y_copy(s):
        return remote(kvh.at[s, oy], kvr.at[s], ys.at[s], yr.at[s], at_y)

    def q_copy(j):
        return remote(qh.at[oy, j], qr.at[j], qs.at[j], qrs.at[j], at_y)

    def spread(origin, s):
        @pl.when(jnp.logical_and(has_right, origin <= line))
        def _():
            z_right(s).start()

        @pl.when(jnp.logical_and(has_left, origin >= line))
        def _():
            z_left(s).start()

        x_copy(s, head).start()
        c_copy(s, head, 0).start()

    for j in range(CHUNKS):
        own[j].wait()
        spread(line, line * CHUNKS + j)
    for copy in loads:
        copy.wait()

    def unit(values):
        mean = jnp.dot((values * values).astype(BF16), mean_mat[...], preferred_element_type=F32)
        return values * lax.rsqrt(mean + EPS)

    lane_w = lax.broadcasted_iota(jnp.int32, (1, width), 1) // size
    scale = jnp.zeros((1, width), F32)
    for h in range(heads):
        scale = jnp.where(lane_w == h, temper_ref[h] * (LOG2E / size), scale)

    def tokens_here(n):
        origin, s = slot_of(n)
        c_copy(s, chead, 0).wait_recv()
        c_copy(s, dhead, 1).wait_recv()

    def project(n):
        origin, s = slot_of(n)
        parts = [tok[s, h].astype(F32) for h in range(count)]
        squares = parts[0] * parts[0]
        for p in parts[1:]:
            squares = squares + p * p
        inv = lax.rsqrt(jnp.sum(squares, axis=-1, keepdims=True) * (1.0 / features) + EPS)
        normed = jnp.concatenate(
            [(parts[h] * inv * gain_ref[:, h * cols:(h + 1) * cols]).astype(BF16) for h in range(count)], axis=1
        )
        keys = unit(jnp.dot(normed, wk[...], preferred_element_type=F32)).astype(BF16)
        values = jnp.dot(normed, wv[...], preferred_element_type=F32).astype(BF16)
        for half in range(2):
            kvh[s, half, 0] = keys[:, half * pair:(half + 1) * pair]
            kvh[s, half, 1] = values[:, half * pair:(half + 1) * pair]
        return normed

    def send_pair(n):
        origin, s = slot_of(n)
        y_copy(s).start()

    def ask(n, normed):
        @pl.when(n < CHUNKS)
        def _():
            query = unit(jnp.dot(normed, wq[...], preferred_element_type=F32))
            query = (query * scale).astype(BF16)
            for half in range(2):
                qh[half, n] = query[:, half * pair:(half + 1) * pair]
            q_copy(n).start()

    low = lax.broadcasted_iota(jnp.int32, (1, pair), 1) < size

    def split_queries():
        for j in range(CHUNKS):
            q_copy(j).wait_recv()
        for side in range(2):
            for j in range(CHUNKS):
                piece = qh[y, j] if side == 0 else qr[j]
                at = side * rows + j * rp
                zero = jnp.zeros_like(piece)
                qm[0, at:at + rp, :] = jnp.where(low, piece, zero)
                qm[1, at:at + rp, :] = jnp.where(low, zero, piece)

    local = rows // BLOCK
    per_chunk = rp // BLOCK
    q_blocks = [order_ref[(line * 2 + side) * local + i] for side in (y, oy) for i in range(local)]
    key_lane = lax.broadcasted_iota(jnp.int32, (1, 2 * rp), 1) // BLOCK

    def pair_here(n):
        origin, s = slot_of(n)
        y_copy(s).wait_recv()

    def fetch(n):
        origin, s = slot_of(n)
        keys = jnp.concatenate([kvh[s, y, 0], kvr[s, 0]], axis=0)
        values = jnp.concatenate([kvh[s, y, 1], kvr[s, 1]], axis=0)
        return keys, values

    def attend(n, keys, values):
        origin, s = slot_of(n)
        first = (s - origin * CHUNKS) * per_chunk
        k_blocks = [order_ref[(origin * 2 + side) * local + first + i] for side in (y, oy) for i in range(per_chunk)]
        masks = []
        for qb in q_blocks:
            mask = jnp.zeros((1, 2 * rp), F32)
            for i, kb in enumerate(k_blocks):
                mask = jnp.where(key_lane == i, (adj_ref[qb, kb] > 0).astype(F32), mask)
            masks.append(mask)
        ones = jnp.ones_like(values)
        for h in range(2):
            mine = jnp.where(low, values, ones) if h == 0 else jnp.where(low, ones, values)
            scores = lax.dot_general(qm[h], keys, (((1,), (1,)), ((), ())), preferred_element_type=F32)
            probs = jnp.concatenate(
                [(jnp.exp2(scores[i * BLOCK:(i + 1) * BLOCK]) * masks[i]).astype(BF16) for i in range(2 * local)], axis=0
            )
            acc[h] += jnp.dot(probs, mine, preferred_element_type=F32)

    def w_columns(h):
        return wo_hbm.at[:, pl.ds(pl.multiple_of(h * cols, cols), cols)]

    def w_rows(h):
        return wall_ref.at[pl.ds(pl.multiple_of(h * width, width), width), :]

    def w_copy(which):
        h, where = ((xhead, at_x), (dhead, at_d), (chead, at_c))[which]
        return remote(w_columns(h), w_rows(head), ws.at[which], wr.at[which], where)

    def w_own():
        return pltpu.make_async_copy(w_columns(head), w_rows(head), wl)

    def step(n, carry):
        away = n // CHUNKS + 1

        @pl.when(line - away >= 0)
        def _():
            s = (line - away) * CHUNKS + n % CHUNKS
            z_right(s).wait_recv()
            spread(line - away, s)

        @pl.when(line + away < depth)
        def _():
            s = (line + away) * CHUNKS + n % CHUNKS
            z_left(s).wait_recv()
            spread(line + away, s)

        @pl.when(n < total)
        def _():
            origin, s = slot_of(n)
            x_copy(s, xhead).wait_recv()
            c_copy(s, xhead, 1).start()

        @pl.when(n == total - 1)
        def _():
            for which in range(3):
                w_copy(which).start()
            w_own().start()

        @pl.when(jnp.logical_and(n >= 1, n < lag))
        def _():
            tokens_here(n - 1)
            normed = project(n - 1)
            send_pair(n - 1)
            ask(n - 1, normed)

        @pl.when(n == lag)
        def _():
            split_queries()

        @pl.when(jnp.logical_and(n >= lag, n <= total))
        def _():
            tokens_here(n - 1)
            pair_here(n - lag)
            keys, values = fetch(n - lag)
            project(n - 1)
            attend(n - lag, keys, values)
            send_pair(n - 1)

        @pl.when(n > total)
        def _():
            pair_here(n - lag)
            attend(n - lag, *fetch(n - lag))

        return carry

    lax.fori_loop(0, total + lag, step, 0)

    tp = rows // TAIL

    def finish(at):
        first, second = acc[0, at:at + tp, :], acc[1, at:at + tp, :]
        weight = pltpu.roll(jnp.where(low, second, first), size, 1)
        return (jnp.where(low, first, second) / weight).astype(BF16)

    def block(h, half, r):
        at = pl.multiple_of((h * 2 + half) * pair, pair)
        return all_ref.at[pl.ds(r * tp, tp), pl.ds(at, pair)]

    def a_copy(r):
        return remote(asend.at[r], abuf.at[y, r], as_.at[r], ar.at[r], at_y)

    def ax_copy(r):
        return remote(abuf.at[y, r], xbuf.at[y, r], axs.at[0, r], axr.at[0, r], at_x)

    def axy_copy(r):
        return remote(asend.at[r], xbuf.at[y, r], axs.at[1, r], axr.at[1, r], at_xy)

    def ac_copy(src, h, half, r, k):
        return remote(src.at[half, r], block(h, half, r), acs.at[k, r], acr.at[k, r], at_c)

    def keep(src, h, half, r, k):
        return pltpu.make_async_copy(src.at[half, r], block(h, half, r), al.at[k, r])

    for r in range(TAIL):
        asend[r] = finish(rows + r * tp)
        axy_copy(r).start()
        a_copy(r).start()
    for r in range(TAIL):
        abuf[y, r] = finish(r * tp)
        ax_copy(r).start()
    for r in range(TAIL):
        ac_copy(abuf, head, y, r, 0).start()
        keep(abuf, head, y, r, 0).start()
    for r in range(TAIL):
        a_copy(r).wait_recv()
        ac_copy(abuf, head, oy, r, 1).start()
        keep(abuf, head, oy, r, 1).start()
    for r in range(TAIL):
        for k, half, copy in ((1, oy, axy_copy), (0, y, ax_copy)):
            copy(r).wait_recv()
            ac_copy(xbuf, xhead, half, r, 2 + k).start()
            keep(xbuf, xhead, half, r, 2 + k).start()

    def drain(n, carry):
        origin, s = slot_of(n)

        @pl.when(jnp.logical_and(has_right, origin <= line))
        def _():
            z_right(s).wait_send()

        @pl.when(jnp.logical_and(has_left, origin >= line))
        def _():
            z_left(s).wait_send()

        x_copy(s, head).wait_send()
        c_copy(s, head, 0).wait_send()
        c_copy(s, xhead, 1).wait_send()
        y_copy(s).wait_send()
        return carry

    lax.fori_loop(0, total, drain, 0)
    for j in range(CHUNKS):
        q_copy(j).wait_send()
    for which in range(3):
        w_copy(which).wait()
    w_own().wait()
    for r in range(TAIL):
        a_copy(r).wait_send()
        ax_copy(r).wait_send()
        axy_copy(r).wait_send()
        for k, half in ((0, y), (1, oy)):
            for base, src, h in ((0, abuf, head), (2, xbuf, xhead)):
                ac_copy(src, h, half, r, base + k).wait()
                keep(src, h, half, r, base + k).wait()


def shards(depth, tokens, gain, w_query, w_key, w_value, w_out, temper, adjacency, order):
    rows, cols = tokens.shape
    features, width = w_query.shape
    count = features // cols
    pair = width // 2
    rp = rows // CHUNKS
    tp = rows // TAIL
    total = depth * CHUNKS
    dma = pltpu.SemaphoreType.DMA
    smem = pl.BlockSpec(memory_space=pltpu.SMEM)
    vmem = pl.BlockSpec(memory_space=pltpu.VMEM)
    hbm = pl.BlockSpec(memory_space=pl.ANY)
    attended, weights = pl.pallas_call(
        functools.partial(kernel, depth),
        out_shape=(
            jax.ShapeDtypeStruct((rows, count * width), BF16),
            jax.ShapeDtypeStruct((count * width, cols), BF16),
        ),
        in_specs=[smem, smem, smem, vmem, hbm, hbm, hbm, hbm, hbm],
        out_specs=(hbm, hbm),
        scratch_shapes=[
            pltpu.VMEM((total, count, rp, cols), BF16),
            pltpu.VMEM((features, width), BF16),
            pltpu.VMEM((features, width), BF16),
            pltpu.VMEM((features, width), BF16),
            pltpu.VMEM((width, width), BF16),
            pltpu.VMEM((total, 2, 2, rp, pair), BF16),
            pltpu.VMEM((total, 2, rp, pair), BF16),
            pltpu.VMEM((2, CHUNKS, rp, pair), BF16),
            pltpu.VMEM((CHUNKS, rp, pair), BF16),
            pltpu.VMEM((2, 2 * rows, pair), BF16),
            pltpu.VMEM((2, 2 * rows, pair), F32),
            pltpu.VMEM((TAIL, tp, pair), BF16),
            pltpu.VMEM((2, TAIL, tp, pair), BF16),
            pltpu.VMEM((2, TAIL, tp, pair), BF16),
            dma((3,)),
            dma((CHUNKS,)),
            dma((2, total)),
            dma((total,)),
            dma((total,)),
            dma((total,)),
            dma((total, 2)),
            dma((total, 2)),
            dma((total,)),
            dma((total,)),
            dma((CHUNKS,)),
            dma((CHUNKS,)),
            dma((TAIL,)),
            dma((TAIL,)),
            dma((2, TAIL)),
            dma((2, TAIL)),
            dma((4, TAIL)),
            dma((4, TAIL)),
            dma((4, TAIL)),
            dma((3,)),
            dma((3,)),
            dma,
        ],
        compiler_params=pltpu.CompilerParams(
            collective_id=0, has_side_effects=True, vmem_limit_bytes=56 * 1024 * 1024
        ),
    )(order, adjacency, temper, gain.reshape(1, features), tokens, w_query, w_key, w_value, w_out)
    return jnp.dot(attended, weights, preferred_element_type=F32).astype(BF16)


def solution(mesh):
    in_specs = (
        P("ctx", "head"),
        P(),
        P(None, "head"),
        P(None, "head"),
        P(None, "head"),
        P("head", None),
        P("head"),
        P(),
        P(),
    )
    out_specs = P("ctx", "head")
    body = functools.partial(shards, mesh.shape["ctx"] // 2)
    return jax.shard_map(body, mesh=mesh, in_specs=in_specs, out_specs=out_specs, check_vma=False)
```

```python
import functools

import jax
import jax.numpy as jnp
from jax import lax
from jax.experimental import pallas as pl
from jax.experimental.pallas import tpu as pltpu
from jax.sharding import PartitionSpec as P

BLOCK = 128
CHUNKS = 2
TAIL = 2
EPS = 1e-06
LOG2E = 1.4426950408889634
MESH = pl.DeviceIdType.MESH
F32 = jnp.float32
BF16 = jnp.bfloat16


def visit(line, depth, n):
    far = depth - 1 - line
    near = jnp.minimum(line, far) * CHUNKS
    p = n - CHUNKS
    paired = p < 2 * near
    t = jnp.where(paired, p // 2, p - near)
    to_left = jnp.where(paired, p % 2 == 0, line > far)
    away = t // CHUNKS + 1
    origin = jnp.where(n < CHUNKS, line, jnp.where(to_left, line - away, line + away))
    return origin, jnp.where(n < CHUNKS, n, t % CHUNKS)


def kernel(
    depth,
    order_ref, adj_ref, temper_ref, gain_ref, tokens_ref, wq_hbm, wk_hbm, wv_hbm, wo_hbm,
    all_ref, wall_ref,
    tok, wq, wk, wv, mean_mat, kvh, kvr, qh, qr, qm, acc, asend, abuf, xbuf,
    w_sem, t_sem, zs, zr, xs, xr, cs, cr, ys, yr, qs, qrs, as_, ar, axs, axr, acs, acr, al, ws, wr, wl,
):
    ctx, head = lax.axis_index("ctx"), lax.axis_index("head")
    line, y = ctx // 2, ctx % 2
    x, c = head // 2, head % 2
    oy, ox, oc = 1 - y, 1 - x, 1 - c
    rows, cols = tokens_ref.shape
    heads = temper_ref.shape[0]
    width = wq.shape[1]
    size = width // heads
    pair = width // 2
    rp = rows // CHUNKS
    total = depth * CHUNKS
    features = wq.shape[0]
    lag = CHUNKS + 2
    has_left, has_right = line > 0, line < depth - 1
    at_left, at_right = (ctx - 2, head), (ctx + 2, head)
    at_y = (line * 2 + oy, head)
    at_x = (ctx, ox * 2 + c)
    at_xy = (line * 2 + oy, ox * 2 + c)
    at_c = (ctx, x * 2 + oc)
    xhead = ox * 2 + c
    chead = x * 2 + oc
    dhead = ox * 2 + oc
    at_d = (ctx, dhead)

    def remote(src, dst, send, recv, where):
        return pltpu.make_async_remote_copy(
            src_ref=src, dst_ref=dst, send_sem=send, recv_sem=recv, device_id=where, device_id_type=MESH
        )

    loads = [
        pltpu.make_async_copy(wk_hbm, wk, w_sem.at[0]),
        pltpu.make_async_copy(wv_hbm, wv, w_sem.at[1]),
        pltpu.make_async_copy(wq_hbm, wq, w_sem.at[2]),
    ]
    count = features // cols
    own = [
        pltpu.make_async_copy(tokens_ref.at[pl.ds(j * rp, rp), :], tok.at[line * CHUNKS + j, head], t_sem.at[j])
        for j in range(CHUNKS)
    ]
    for copy in own + loads:
        copy.start()

    barrier = pltpu.get_barrier_semaphore()
    for where in (at_y, at_x, at_c, at_d, at_xy):
        pl.semaphore_signal(barrier, inc=1, device_id=where, device_id_type=MESH)

    @pl.when(has_left)
    def _():
        pl.semaphore_signal(barrier, inc=1, device_id=at_left, device_id_type=MESH)

    @pl.when(has_right)
    def _():
        pl.semaphore_signal(barrier, inc=1, device_id=at_right, device_id_type=MESH)

    row_id = lax.broadcasted_iota(jnp.int32, (width, width), 0) // size
    col_id = lax.broadcasted_iota(jnp.int32, (width, width), 1) // size
    mean_mat[...] = jnp.where(row_id == col_id, 1.0 / size, 0.0).astype(BF16)
    acc[...] = jnp.zeros_like(acc)
    pl.semaphore_wait(barrier, 5 + has_left.astype(jnp.int32) + has_right.astype(jnp.int32))

    def slot_of(n):
        origin, j = visit(line, depth, n)
        return origin, origin * CHUNKS + j

    def z_right(s):
        return remote(tok.at[s, head], tok.at[s, head], zs.at[1, s], zr.at[s], at_right)

    def z_left(s):
        return remote(tok.at[s, head], tok.at[s, head], zs.at[0, s], zr.at[s], at_left)

    def x_copy(s, h):
        return remote(tok.at[s, h], tok.at[s, h], xs.at[s], xr.at[s], at_x)

    def c_copy(s, h, which):
        return remote(tok.at[s, h], tok.at[s, h], cs.at[s, which], cr.at[s, which], at_c)

    def y_copy(s):
        return remote(kvh.at[s, oy], kvr.at[s], ys.at[s], yr.at[s], at_y)

    def q_copy(j):
        return remote(qh.at[oy, j], qr.at[j], qs.at[j], qrs.at[j], at_y)

    def spread(origin, s):
        @pl.when(jnp.logical_and(has_right, origin <= line))
        def _():
            z_right(s).start()

        @pl.when(jnp.logical_and(has_left, origin >= line))
        def _():
            z_left(s).start()

        x_copy(s, head).start()
        c_copy(s, head, 0).start()

    for j in range(CHUNKS):
        own[j].wait()
        spread(line, line * CHUNKS + j)
    for copy in loads:
        copy.wait()

    def unit(values):
        mean = jnp.dot((values * values).astype(BF16), mean_mat[...], preferred_element_type=F32)
        return values * lax.rsqrt(mean + EPS)

    lane_w = lax.broadcasted_iota(jnp.int32, (1, width), 1) // size
    scale = jnp.zeros((1, width), F32)
    for h in range(heads):
        scale = jnp.where(lane_w == h, temper_ref[h] * (LOG2E / size), scale)

    def tokens_here(n):
        origin, s = slot_of(n)
        c_copy(s, chead, 0).wait_recv()
        c_copy(s, dhead, 1).wait_recv()

    def project(n):
        origin, s = slot_of(n)
        parts = [tok[s, h].astype(F32) for h in range(count)]
        squares = parts[0] * parts[0]
        for p in parts[1:]:
            squares = squares + p * p
        inv = lax.rsqrt(jnp.sum(squares, axis=-1, keepdims=True) * (1.0 / features) + EPS)
        normed = jnp.concatenate(
            [(parts[h] * inv * gain_ref[:, h * cols:(h + 1) * cols]).astype(BF16) for h in range(count)], axis=1
        )
        keys = unit(jnp.dot(normed, wk[...], preferred_element_type=F32)).astype(BF16)
        values = jnp.dot(normed, wv[...], preferred_element_type=F32).astype(BF16)
        for half in range(2):
            kvh[s, half, 0] = keys[:, half * pair:(half + 1) * pair]
            kvh[s, half, 1] = values[:, half * pair:(half + 1) * pair]
        return normed

    def send_pair(n):
        origin, s = slot_of(n)
        y_copy(s).start()

    def ask(n, normed):
        @pl.when(n < CHUNKS)
        def _():
            query = unit(jnp.dot(normed, wq[...], preferred_element_type=F32))
            query = (query * scale).astype(BF16)
            for half in range(2):
                qh[half, n] = query[:, half * pair:(half + 1) * pair]
            q_copy(n).start()

    low = lax.broadcasted_iota(jnp.int32, (1, pair), 1) < size

    def split_queries():
        for j in range(CHUNKS):
            q_copy(j).wait_recv()
        for side in range(2):
            for j in range(CHUNKS):
                piece = qh[y, j] if side == 0 else qr[j]
                at = side * rows + j * rp
                zero = jnp.zeros_like(piece)
                qm[0, at:at + rp, :] = jnp.where(low, piece, zero)
                qm[1, at:at + rp, :] = jnp.where(low, zero, piece)

    local = rows // BLOCK
    per_chunk = rp // BLOCK
    q_blocks = [order_ref[(line * 2 + side) * local + i] for side in (y, oy) for i in range(local)]
    key_lane = lax.broadcasted_iota(jnp.int32, (1, 2 * rp), 1) // BLOCK

    def pair_here(n):
        origin, s = slot_of(n)
        y_copy(s).wait_recv()

    def fetch(n):
        origin, s = slot_of(n)
        keys = jnp.concatenate([kvh[s, y, 0], kvr[s, 0]], axis=0)
        values = jnp.concatenate([kvh[s, y, 1], kvr[s, 1]], axis=0)
        return keys, values

    def attend(n, keys, values, sides):
        origin, s = slot_of(n)
        first = (s - origin * CHUNKS) * per_chunk
        k_blocks = [order_ref[(origin * 2 + side) * local + first + i] for side in (y, oy) for i in range(per_chunk)]
        masks = []
        for qb in q_blocks:
            mask = jnp.zeros((1, 2 * rp), F32)
            for i, kb in enumerate(k_blocks):
                mask = jnp.where(key_lane == i, (adj_ref[qb, kb] > 0).astype(F32), mask)
            masks.append(mask)
        ones = jnp.ones_like(values)
        at, to = sides[0] * rows, (sides[-1] + 1) * rows
        for h in range(2):
            mine = jnp.where(low, values, ones) if h == 0 else jnp.where(low, ones, values)
            scores = lax.dot_general(qm[h, at:to, :], keys, (((1,), (1,)), ((), ())), preferred_element_type=F32)
            probs = jnp.concatenate(
                [
                    (jnp.exp2(scores[i * BLOCK:(i + 1) * BLOCK]) * masks[at // BLOCK + i]).astype(BF16)
                    for i in range((to - at) // BLOCK)
                ],
                axis=0,
            )
            acc[h, at:to, :] += jnp.dot(probs, mine, preferred_element_type=F32)

    def w_columns(h):
        return wo_hbm.at[:, pl.ds(pl.multiple_of(h * cols, cols), cols)]

    def w_rows(h):
        return wall_ref.at[pl.ds(pl.multiple_of(h * width, width), width), :]

    def w_copy(which):
        h, where = ((xhead, at_x), (dhead, at_d), (chead, at_c))[which]
        return remote(w_columns(h), w_rows(head), ws.at[which], wr.at[which], where)

    def w_own():
        return pltpu.make_async_copy(w_columns(head), w_rows(head), wl)

    def step(n, carry):
        away = n // CHUNKS + 1

        @pl.when(line - away >= 0)
        def _():
            s = (line - away) * CHUNKS + n % CHUNKS
            z_right(s).wait_recv()
            spread(line - away, s)

        @pl.when(line + away < depth)
        def _():
            s = (line + away) * CHUNKS + n % CHUNKS
            z_left(s).wait_recv()
            spread(line + away, s)

        @pl.when(n < total)
        def _():
            origin, s = slot_of(n)
            x_copy(s, xhead).wait_recv()
            c_copy(s, xhead, 1).start()

        @pl.when(n == total - 1)
        def _():
            for which in range(3):
                w_copy(which).start()
            w_own().start()

        @pl.when(jnp.logical_or(jnp.logical_and(n >= 1, n < lag), n == total))
        def _():
            tokens_here(n - 1)
            normed = project(n - 1)
            send_pair(n - 1)
            ask(n - 1, normed)

        @pl.when(n == lag)
        def _():
            split_queries()

        @pl.when(jnp.logical_and(n >= lag, n < total))
        def _():
            tokens_here(n - 1)
            pair_here(n - lag)
            keys, values = fetch(n - lag)
            project(n - 1)
            attend(n - lag, keys, values, (0, 1))
            send_pair(n - 1)

        @pl.when(n >= total)
        def _():
            pair_here(n - lag)
            attend(n - lag, *fetch(n - lag), (0, 1))

        return carry

    lax.fori_loop(0, total + lag - 1, step, 0)

    tp = rows // TAIL

    def finish(at):
        first, second = acc[0, at:at + tp, :], acc[1, at:at + tp, :]
        weight = pltpu.roll(jnp.where(low, second, first), size, 1)
        return (jnp.where(low, first, second) / weight).astype(BF16)

    def block(h, half, r):
        at = pl.multiple_of((h * 2 + half) * pair, pair)
        return all_ref.at[pl.ds(r * tp, tp), pl.ds(at, pair)]

    def a_copy(r):
        return remote(asend.at[r], abuf.at[y, r], as_.at[r], ar.at[r], at_y)

    def ax_copy(r):
        return remote(abuf.at[y, r], xbuf.at[y, r], axs.at[0, r], axr.at[0, r], at_x)

    def axy_copy(r):
        return remote(asend.at[r], xbuf.at[y, r], axs.at[1, r], axr.at[1, r], at_xy)

    def ac_copy(src, h, half, r, k):
        return remote(src.at[half, r], block(h, half, r), acs.at[k, r], acr.at[k, r], at_c)

    def keep(src, h, half, r, k):
        return pltpu.make_async_copy(src.at[half, r], block(h, half, r), al.at[k, r])

    pair_here(total - 1)
    keys, values = fetch(total - 1)
    attend(total - 1, keys, values, (1,))
    for r in range(TAIL):
        asend[r] = finish(rows + r * tp)
        axy_copy(r).start()
        a_copy(r).start()
    attend(total - 1, keys, values, (0,))
    for r in range(TAIL):
        abuf[y, r] = finish(r * tp)
        ax_copy(r).start()
    for r in range(TAIL):
        ac_copy(abuf, head, y, r, 0).start()
        keep(abuf, head, y, r, 0).start()

    def drain(n, carry):
        origin, s = slot_of(n)

        @pl.when(jnp.logical_and(has_right, origin <= line))
        def _():
            z_right(s).wait_send()

        @pl.when(jnp.logical_and(has_left, origin >= line))
        def _():
            z_left(s).wait_send()

        x_copy(s, head).wait_send()
        c_copy(s, head, 0).wait_send()
        c_copy(s, xhead, 1).wait_send()
        y_copy(s).wait_send()
        return carry

    lax.fori_loop(0, total, drain, 0)
    for j in range(CHUNKS):
        q_copy(j).wait_send()
    for r in range(TAIL):
        a_copy(r).wait_recv()
        ac_copy(abuf, head, oy, r, 1).start()
        keep(abuf, head, oy, r, 1).start()
    for r in range(TAIL):
        for k, half, copy in ((1, oy, axy_copy), (0, y, ax_copy)):
            copy(r).wait_recv()
            ac_copy(xbuf, xhead, half, r, 2 + k).start()
            keep(xbuf, xhead, half, r, 2 + k).start()

    for which in range(3):
        w_copy(which).wait()
    w_own().wait()
    for r in range(TAIL):
        a_copy(r).wait_send()
        ax_copy(r).wait_send()
        axy_copy(r).wait_send()
        for k, half in ((0, y), (1, oy)):
            for base, src, h in ((0, abuf, head), (2, xbuf, xhead)):
                ac_copy(src, h, half, r, base + k).wait()
                keep(src, h, half, r, base + k).wait()


def shards(depth, tokens, gain, w_query, w_key, w_value, w_out, temper, adjacency, order):
    rows, cols = tokens.shape
    features, width = w_query.shape
    count = features // cols
    pair = width // 2
    rp = rows // CHUNKS
    tp = rows // TAIL
    total = depth * CHUNKS
    dma = pltpu.SemaphoreType.DMA
    smem = pl.BlockSpec(memory_space=pltpu.SMEM)
    vmem = pl.BlockSpec(memory_space=pltpu.VMEM)
    hbm = pl.BlockSpec(memory_space=pl.ANY)
    attended, weights = pl.pallas_call(
        functools.partial(kernel, depth),
        out_shape=(
            jax.ShapeDtypeStruct((rows, count * width), BF16),
            jax.ShapeDtypeStruct((count * width, cols), BF16),
        ),
        in_specs=[smem, smem, smem, vmem, hbm, hbm, hbm, hbm, hbm],
        out_specs=(hbm, hbm),
        scratch_shapes=[
            pltpu.VMEM((total, count, rp, cols), BF16),
            pltpu.VMEM((features, width), BF16),
            pltpu.VMEM((features, width), BF16),
            pltpu.VMEM((features, width), BF16),
            pltpu.VMEM((width, width), BF16),
            pltpu.VMEM((total, 2, 2, rp, pair), BF16),
            pltpu.VMEM((total, 2, rp, pair), BF16),
            pltpu.VMEM((2, CHUNKS, rp, pair), BF16),
            pltpu.VMEM((CHUNKS, rp, pair), BF16),
            pltpu.VMEM((2, 2 * rows, pair), BF16),
            pltpu.VMEM((2, 2 * rows, pair), F32),
            pltpu.VMEM((TAIL, tp, pair), BF16),
            pltpu.VMEM((2, TAIL, tp, pair), BF16),
            pltpu.VMEM((2, TAIL, tp, pair), BF16),
            dma((3,)),
            dma((CHUNKS,)),
            dma((2, total)),
            dma((total,)),
            dma((total,)),
            dma((total,)),
            dma((total, 2)),
            dma((total, 2)),
            dma((total,)),
            dma((total,)),
            dma((CHUNKS,)),
            dma((CHUNKS,)),
            dma((TAIL,)),
            dma((TAIL,)),
            dma((2, TAIL)),
            dma((2, TAIL)),
            dma((4, TAIL)),
            dma((4, TAIL)),
            dma((4, TAIL)),
            dma((3,)),
            dma((3,)),
            dma,
        ],
        compiler_params=pltpu.CompilerParams(
            collective_id=0, has_side_effects=True, vmem_limit_bytes=56 * 1024 * 1024
        ),
    )(order, adjacency, temper, gain.reshape(1, features), tokens, w_query, w_key, w_value, w_out)
    return jnp.dot(attended, weights, preferred_element_type=F32).astype(BF16)


def solution(mesh):
    in_specs = (
        P("ctx", "head"),
        P(),
        P(None, "head"),
        P(None, "head"),
        P(None, "head"),
        P("head", None),
        P("head"),
        P(),
        P(),
    )
    out_specs = P("ctx", "head")
    body = functools.partial(shards, mesh.shape["ctx"] // 2)
    return jax.shard_map(body, mesh=mesh, in_specs=in_specs, out_specs=out_specs, check_vma=False)
```

```python
import functools

import jax
import jax.numpy as jnp
from jax import lax
from jax.experimental import pallas as pl
from jax.experimental.pallas import tpu as pltpu
from jax.sharding import PartitionSpec as P

BLOCK = 128
CHUNKS = 2
TAIL = 2
EPS = 1e-06
LOG2E = 1.4426950408889634
MESH = pl.DeviceIdType.MESH
F32 = jnp.float32
BF16 = jnp.bfloat16


def visit(line, depth, n):
    far = depth - 1 - line
    near = jnp.minimum(line, far) * CHUNKS
    p = n - CHUNKS
    paired = p < 2 * near
    t = jnp.where(paired, p // 2, p - near)
    to_left = jnp.where(paired, p % 2 == 0, line > far)
    away = t // CHUNKS + 1
    origin = jnp.where(n < CHUNKS, line, jnp.where(to_left, line - away, line + away))
    return origin, jnp.where(n < CHUNKS, n, t % CHUNKS)


def group_of(depth):
    return 4 if depth % 4 == 0 else 2 if depth % 2 == 0 else 1


def kernel(
    depth,
    order_ref, adj_ref, temper_ref, gain_ref, tokens_ref, wq_hbm, wk_hbm, wv_hbm, wo_hbm,
    all_ref, wall_ref,
    tok, wq, wk, wv, mean_mat, kvh, kvr, qh, qr, qm, acc, asend, abuf, xbuf,
    w_sem, t_sem, zs, zr, xs, xr, cs, cr, ys, yr, qs, qrs, as_, ar, axs, axr, acs, acr, al, ws, wr, wl, wzs, wzr,
):
    ctx, head = lax.axis_index("ctx"), lax.axis_index("head")
    line, y = ctx // 2, ctx % 2
    x, c = head // 2, head % 2
    oy, ox, oc = 1 - y, 1 - x, 1 - c
    rows, cols = tokens_ref.shape
    heads = temper_ref.shape[0]
    width = wq.shape[1]
    size = width // heads
    pair = width // 2
    rp = rows // CHUNKS
    total = depth * CHUNKS
    features = wq.shape[0]
    lag = CHUNKS + 2
    has_left, has_right = line > 0, line < depth - 1
    at_left, at_right = (ctx - 2, head), (ctx + 2, head)
    at_y = (line * 2 + oy, head)
    at_x = (ctx, ox * 2 + c)
    at_xy = (line * 2 + oy, ox * 2 + c)
    at_c = (ctx, x * 2 + oc)
    xhead = ox * 2 + c
    chead = x * 2 + oc
    dhead = ox * 2 + oc
    at_d = (ctx, dhead)
    group = group_of(depth)
    base, place = line // group * group, line % group
    share = width // group

    def peer(d):
        return ((base + (place + d) % group) * 2 + y, head)


    def remote(src, dst, send, recv, where):
        return pltpu.make_async_remote_copy(
            src_ref=src, dst_ref=dst, send_sem=send, recv_sem=recv, device_id=where, device_id_type=MESH
        )

    loads = [
        pltpu.make_async_copy(wk_hbm, wk, w_sem.at[0]),
        pltpu.make_async_copy(wv_hbm, wv, w_sem.at[1]),
        pltpu.make_async_copy(wq_hbm, wq, w_sem.at[2]),
    ]
    count = features // cols
    own = [
        pltpu.make_async_copy(tokens_ref.at[pl.ds(j * rp, rp), :], tok.at[line * CHUNKS + j, head], t_sem.at[j])
        for j in range(CHUNKS)
    ]
    for copy in own + loads:
        copy.start()

    barrier = pltpu.get_barrier_semaphore()
    for where in [at_y, at_x, at_c, at_d, at_xy] + [peer(d) for d in range(1, group)]:
        pl.semaphore_signal(barrier, inc=1, device_id=where, device_id_type=MESH)

    @pl.when(has_left)
    def _():
        pl.semaphore_signal(barrier, inc=1, device_id=at_left, device_id_type=MESH)

    @pl.when(has_right)
    def _():
        pl.semaphore_signal(barrier, inc=1, device_id=at_right, device_id_type=MESH)

    row_id = lax.broadcasted_iota(jnp.int32, (width, width), 0) // size
    col_id = lax.broadcasted_iota(jnp.int32, (width, width), 1) // size
    mean_mat[...] = jnp.where(row_id == col_id, 1.0 / size, 0.0).astype(BF16)
    acc[...] = jnp.zeros_like(acc)
    pl.semaphore_wait(barrier, 4 + group + has_left.astype(jnp.int32) + has_right.astype(jnp.int32))

    def slot_of(n):
        origin, j = visit(line, depth, n)
        return origin, origin * CHUNKS + j

    def z_right(s):
        return remote(tok.at[s, head], tok.at[s, head], zs.at[1, s], zr.at[s], at_right)

    def z_left(s):
        return remote(tok.at[s, head], tok.at[s, head], zs.at[0, s], zr.at[s], at_left)

    def x_copy(s, h):
        return remote(tok.at[s, h], tok.at[s, h], xs.at[s], xr.at[s], at_x)

    def c_copy(s, h, which):
        return remote(tok.at[s, h], tok.at[s, h], cs.at[s, which], cr.at[s, which], at_c)

    def y_copy(s):
        return remote(kvh.at[s, oy], kvr.at[s], ys.at[s], yr.at[s], at_y)

    def q_copy(j):
        return remote(qh.at[oy, j], qr.at[j], qs.at[j], qrs.at[j], at_y)

    def spread(origin, s):
        @pl.when(jnp.logical_and(has_right, origin <= line))
        def _():
            z_right(s).start()

        @pl.when(jnp.logical_and(has_left, origin >= line))
        def _():
            z_left(s).start()

        x_copy(s, head).start()
        c_copy(s, head, 0).start()

    for j in range(CHUNKS):
        own[j].wait()
        spread(line, line * CHUNKS + j)
    for copy in loads:
        copy.wait()

    def unit(values):
        mean = jnp.dot((values * values).astype(BF16), mean_mat[...], preferred_element_type=F32)
        return values * lax.rsqrt(mean + EPS)

    lane_w = lax.broadcasted_iota(jnp.int32, (1, width), 1) // size
    scale = jnp.zeros((1, width), F32)
    for h in range(heads):
        scale = jnp.where(lane_w == h, temper_ref[h] * (LOG2E / size), scale)

    def tokens_here(n):
        origin, s = slot_of(n)
        c_copy(s, chead, 0).wait_recv()
        c_copy(s, dhead, 1).wait_recv()

    def project(n):
        origin, s = slot_of(n)
        parts = [tok[s, h].astype(F32) for h in range(count)]
        squares = parts[0] * parts[0]
        for p in parts[1:]:
            squares = squares + p * p
        inv = lax.rsqrt(jnp.sum(squares, axis=-1, keepdims=True) * (1.0 / features) + EPS)
        normed = jnp.concatenate(
            [(parts[h] * inv * gain_ref[:, h * cols:(h + 1) * cols]).astype(BF16) for h in range(count)], axis=1
        )
        keys = unit(jnp.dot(normed, wk[...], preferred_element_type=F32)).astype(BF16)
        values = jnp.dot(normed, wv[...], preferred_element_type=F32).astype(BF16)
        for half in range(2):
            kvh[s, half, 0] = keys[:, half * pair:(half + 1) * pair]
            kvh[s, half, 1] = values[:, half * pair:(half + 1) * pair]
        return normed

    def send_pair(n):
        origin, s = slot_of(n)
        y_copy(s).start()

    def ask(n, normed):
        @pl.when(n < CHUNKS)
        def _():
            query = unit(jnp.dot(normed, wq[...], preferred_element_type=F32))
            query = (query * scale).astype(BF16)
            for half in range(2):
                qh[half, n] = query[:, half * pair:(half + 1) * pair]
            q_copy(n).start()

    low = lax.broadcasted_iota(jnp.int32, (1, pair), 1) < size

    def split_queries():
        for j in range(CHUNKS):
            q_copy(j).wait_recv()
        for side in range(2):
            for j in range(CHUNKS):
                piece = qh[y, j] if side == 0 else qr[j]
                at = side * rows + j * rp
                zero = jnp.zeros_like(piece)
                qm[0, at:at + rp, :] = jnp.where(low, piece, zero)
                qm[1, at:at + rp, :] = jnp.where(low, zero, piece)

    local = rows // BLOCK
    per_chunk = rp // BLOCK
    q_blocks = [order_ref[(line * 2 + side) * local + i] for side in (y, oy) for i in range(local)]
    key_lane = lax.broadcasted_iota(jnp.int32, (1, 2 * rp), 1) // BLOCK

    def pair_here(n):
        origin, s = slot_of(n)
        y_copy(s).wait_recv()

    def fetch(n):
        origin, s = slot_of(n)
        keys = jnp.concatenate([kvh[s, y, 0], kvr[s, 0]], axis=0)
        values = jnp.concatenate([kvh[s, y, 1], kvr[s, 1]], axis=0)
        return keys, values

    def attend(n, keys, values, sides):
        origin, s = slot_of(n)
        first = (s - origin * CHUNKS) * per_chunk
        k_blocks = [order_ref[(origin * 2 + side) * local + first + i] for side in (y, oy) for i in range(per_chunk)]
        masks = []
        for qb in q_blocks:
            mask = jnp.zeros((1, 2 * rp), F32)
            for i, kb in enumerate(k_blocks):
                mask = jnp.where(key_lane == i, (adj_ref[qb, kb] > 0).astype(F32), mask)
            masks.append(mask)
        ones = jnp.ones_like(values)
        at, to = sides[0] * rows, (sides[-1] + 1) * rows
        for h in range(2):
            mine = jnp.where(low, values, ones) if h == 0 else jnp.where(low, ones, values)
            scores = lax.dot_general(qm[h, at:to, :], keys, (((1,), (1,)), ((), ())), preferred_element_type=F32)
            probs = jnp.concatenate(
                [
                    (jnp.exp2(scores[i * BLOCK:(i + 1) * BLOCK]) * masks[at // BLOCK + i]).astype(BF16)
                    for i in range((to - at) // BLOCK)
                ],
                axis=0,
            )
            acc[h, at:to, :] += jnp.dot(probs, mine, preferred_element_type=F32)

    def w_columns(h):
        return wo_hbm.at[:, pl.ds(pl.multiple_of(h * cols, cols), cols)]

    def w_rows(h):
        return wall_ref.at[pl.ds(pl.multiple_of(h * width, width), width), :]

    def w_piece(h, part):
        return wall_ref.at[pl.ds(pl.multiple_of(h * width + part * share, share), share), :]

    def w_copy(which):
        h, where = ((xhead, at_x), (dhead, at_d))[which]
        source = wo_hbm.at[
            pl.ds(pl.multiple_of(place * share, share), share), pl.ds(pl.multiple_of(h * cols, cols), cols)
        ]
        return remote(source, w_piece(head, place), ws.at[which], wr.at[which], where)

    def w_core():
        return remote(w_columns(chead), w_rows(head), ws.at[2], wr.at[2], at_c)

    def w_along(d, which):
        h = (xhead, dhead)[which]
        piece = w_piece(h, place)
        return remote(piece, piece, wzs.at[d - 1, which], wzr.at[d - 1, which], peer(d))

    def w_own():
        return pltpu.make_async_copy(w_columns(head), w_rows(head), wl)

    def step(n, carry):
        away = n // CHUNKS + 1

        @pl.when(line - away >= 0)
        def _():
            s = (line - away) * CHUNKS + n % CHUNKS
            z_right(s).wait_recv()
            spread(line - away, s)

        @pl.when(line + away < depth)
        def _():
            s = (line + away) * CHUNKS + n % CHUNKS
            z_left(s).wait_recv()
            spread(line + away, s)

        @pl.when(n < total)
        def _():
            origin, s = slot_of(n)
            x_copy(s, xhead).wait_recv()
            c_copy(s, xhead, 1).start()

        @pl.when(n == 1)
        def _():
            w_copy(0).start()
            w_copy(1).start()
            w_core().start()
            w_own().start()

        @pl.when(n == total - 2)
        def _():
            for which in range(2):
                w_copy(which).wait_recv()
                for d in range(1, group):
                    w_along(d, which).start()

        @pl.when(jnp.logical_or(jnp.logical_and(n >= 1, n < lag), n == total))
        def _():
            tokens_here(n - 1)
            normed = project(n - 1)
            send_pair(n - 1)
            ask(n - 1, normed)

        @pl.when(n == lag)
        def _():
            split_queries()

        @pl.when(jnp.logical_and(n >= lag, n < total))
        def _():
            tokens_here(n - 1)
            pair_here(n - lag)
            keys, values = fetch(n - lag)
            project(n - 1)
            attend(n - lag, keys, values, (0, 1))
            send_pair(n - 1)

        @pl.when(n >= total)
        def _():
            pair_here(n - lag)
            attend(n - lag, *fetch(n - lag), (0, 1))

        return carry

    lax.fori_loop(0, total + lag - 1, step, 0)

    tp = rows // TAIL

    def finish(at):
        first, second = acc[0, at:at + tp, :], acc[1, at:at + tp, :]
        weight = pltpu.roll(jnp.where(low, second, first), size, 1)
        return (jnp.where(low, first, second) / weight).astype(BF16)

    def block(h, half, r):
        at = pl.multiple_of((h * 2 + half) * pair, pair)
        return all_ref.at[pl.ds(r * tp, tp), pl.ds(at, pair)]

    def a_copy(r):
        return remote(asend.at[r], abuf.at[y, r], as_.at[r], ar.at[r], at_y)

    def ax_copy(r):
        return remote(abuf.at[y, r], xbuf.at[y, r], axs.at[0, r], axr.at[0, r], at_x)

    def axy_copy(r):
        return remote(asend.at[r], xbuf.at[y, r], axs.at[1, r], axr.at[1, r], at_xy)

    def ac_copy(src, h, half, r, k):
        return remote(src.at[half, r], block(h, half, r), acs.at[k, r], acr.at[k, r], at_c)

    def keep(src, h, half, r, k):
        return pltpu.make_async_copy(src.at[half, r], block(h, half, r), al.at[k, r])

    pair_here(total - 1)
    keys, values = fetch(total - 1)
    attend(total - 1, keys, values, (1,))
    for r in range(TAIL):
        asend[r] = finish(rows + r * tp)
        axy_copy(r).start()
        a_copy(r).start()
    attend(total - 1, keys, values, (0,))
    for r in range(TAIL):
        abuf[y, r] = finish(r * tp)
        ax_copy(r).start()
    for r in range(TAIL):
        ac_copy(abuf, head, y, r, 0).start()
        keep(abuf, head, y, r, 0).start()

    def drain(n, carry):
        origin, s = slot_of(n)

        @pl.when(jnp.logical_and(has_right, origin <= line))
        def _():
            z_right(s).wait_send()

        @pl.when(jnp.logical_and(has_left, origin >= line))
        def _():
            z_left(s).wait_send()

        x_copy(s, head).wait_send()
        c_copy(s, head, 0).wait_send()
        c_copy(s, xhead, 1).wait_send()
        y_copy(s).wait_send()
        return carry

    lax.fori_loop(0, total, drain, 0)
    for j in range(CHUNKS):
        q_copy(j).wait_send()
    for r in range(TAIL):
        a_copy(r).wait_recv()
        ac_copy(abuf, head, oy, r, 1).start()
        keep(abuf, head, oy, r, 1).start()
    for r in range(TAIL):
        for k, half, copy in ((1, oy, axy_copy), (0, y, ax_copy)):
            copy(r).wait_recv()
            ac_copy(xbuf, xhead, half, r, 2 + k).start()
            keep(xbuf, xhead, half, r, 2 + k).start()

    for which in range(2):
        w_copy(which).wait_send()
        for d in range(1, group):
            w_along(d, which).wait()
    w_core().wait()
    w_own().wait()
    for r in range(TAIL):
        a_copy(r).wait_send()
        ax_copy(r).wait_send()
        axy_copy(r).wait_send()
        for k, half in ((0, y), (1, oy)):
            for base, src, h in ((0, abuf, head), (2, xbuf, xhead)):
                ac_copy(src, h, half, r, base + k).wait()
                keep(src, h, half, r, base + k).wait()


def shards(depth, tokens, gain, w_query, w_key, w_value, w_out, temper, adjacency, order):
    rows, cols = tokens.shape
    features, width = w_query.shape
    count = features // cols
    pair = width // 2
    rp = rows // CHUNKS
    tp = rows // TAIL
    total = depth * CHUNKS
    dma = pltpu.SemaphoreType.DMA
    smem = pl.BlockSpec(memory_space=pltpu.SMEM)
    vmem = pl.BlockSpec(memory_space=pltpu.VMEM)
    hbm = pl.BlockSpec(memory_space=pl.ANY)
    attended, weights = pl.pallas_call(
        functools.partial(kernel, depth),
        out_shape=(
            jax.ShapeDtypeStruct((rows, count * width), BF16),
            jax.ShapeDtypeStruct((count * width, cols), BF16),
        ),
        in_specs=[smem, smem, smem, vmem, hbm, hbm, hbm, hbm, hbm],
        out_specs=(hbm, hbm),
        scratch_shapes=[
            pltpu.VMEM((total, count, rp, cols), BF16),
            pltpu.VMEM((features, width), BF16),
            pltpu.VMEM((features, width), BF16),
            pltpu.VMEM((features, width), BF16),
            pltpu.VMEM((width, width), BF16),
            pltpu.VMEM((total, 2, 2, rp, pair), BF16),
            pltpu.VMEM((total, 2, rp, pair), BF16),
            pltpu.VMEM((2, CHUNKS, rp, pair), BF16),
            pltpu.VMEM((CHUNKS, rp, pair), BF16),
            pltpu.VMEM((2, 2 * rows, pair), BF16),
            pltpu.VMEM((2, 2 * rows, pair), F32),
            pltpu.VMEM((TAIL, tp, pair), BF16),
            pltpu.VMEM((2, TAIL, tp, pair), BF16),
            pltpu.VMEM((2, TAIL, tp, pair), BF16),
            dma((3,)),
            dma((CHUNKS,)),
            dma((2, total)),
            dma((total,)),
            dma((total,)),
            dma((total,)),
            dma((total, 2)),
            dma((total, 2)),
            dma((total,)),
            dma((total,)),
            dma((CHUNKS,)),
            dma((CHUNKS,)),
            dma((TAIL,)),
            dma((TAIL,)),
            dma((2, TAIL)),
            dma((2, TAIL)),
            dma((4, TAIL)),
            dma((4, TAIL)),
            dma((4, TAIL)),
            dma((3,)),
            dma((3,)),
            dma,
            dma((max(group_of(depth) - 1, 1), 2)),
            dma((max(group_of(depth) - 1, 1), 2)),
        ],
        compiler_params=pltpu.CompilerParams(
            collective_id=0, has_side_effects=True, vmem_limit_bytes=56 * 1024 * 1024
        ),
    )(order, adjacency, temper, gain.reshape(1, features), tokens, w_query, w_key, w_value, w_out)
    return jnp.dot(attended, weights, preferred_element_type=F32).astype(BF16)


def solution(mesh):
    in_specs = (
        P("ctx", "head"),
        P(),
        P(None, "head"),
        P(None, "head"),
        P(None, "head"),
        P("head", None),
        P("head"),
        P(),
        P(),
    )
    out_specs = P("ctx", "head")
    body = functools.partial(shards, mesh.shape["ctx"] // 2)
    return jax.shard_map(body, mesh=mesh, in_specs=in_specs, out_specs=out_specs, check_vma=False)
```

```python
import functools

import jax
import jax.numpy as jnp
from jax import lax
from jax.experimental import pallas as pl
from jax.experimental.pallas import tpu as pltpu
from jax.sharding import PartitionSpec as P

BLOCK = 128
CHUNKS = 2
TAIL = 2
EPS = 1e-06
LOG2E = 1.4426950408889634
MESH = pl.DeviceIdType.MESH
F32 = jnp.float32
BF16 = jnp.bfloat16


def visit(line, depth, n):
    far = depth - 1 - line
    near = jnp.minimum(line, far) * CHUNKS
    p = n - CHUNKS
    paired = p < 2 * near
    t = jnp.where(paired, p // 2, p - near)
    to_left = jnp.where(paired, p % 2 == 0, line > far)
    away = t // CHUNKS + 1
    origin = jnp.where(n < CHUNKS, line, jnp.where(to_left, line - away, line + away))
    return origin, jnp.where(n < CHUNKS, n, t % CHUNKS)


def kernel(
    depth,
    order_ref, adj_ref, temper_ref, gain_ref, tokens_ref, wq_hbm, wk_hbm, wv_hbm, wo_hbm,
    all_ref, wall_ref,
    tok, wq, wk, wv, mean_mat, kvh, kvr, qh, qr, qm, acc, asend, abuf, xbuf,
    w_sem, t_sem, zs, zes, zr, xs, xr, cs, cr, ys, yr, qs, qrs, as_, ar, axs, axr, acs, acr, al, ws, wr, wl,
):
    ctx, head = lax.axis_index("ctx"), lax.axis_index("head")
    line, y = ctx // 2, ctx % 2
    x, c = head // 2, head % 2
    oy, ox, oc = 1 - y, 1 - x, 1 - c
    rows, cols = tokens_ref.shape
    heads = temper_ref.shape[0]
    width = wq.shape[1]
    size = width // heads
    pair = width // 2
    rp = rows // CHUNKS
    total = depth * CHUNKS
    features = wq.shape[0]
    lag = CHUNKS + 2
    has_left, has_right = line > 0, line < depth - 1
    at_left, at_right = (ctx - 2, head), (ctx + 2, head)
    at_y = (line * 2 + oy, head)
    at_x = (ctx, ox * 2 + c)
    at_xy = (line * 2 + oy, ox * 2 + c)
    at_c = (ctx, x * 2 + oc)
    xhead = ox * 2 + c
    chead = x * 2 + oc
    dhead = ox * 2 + oc
    at_d = (ctx, dhead)
    is_end = jnp.logical_or(line == 0, line == depth - 1)

    def on_line(d):
        return ((line + d) % depth * 2 + y, head)


    def remote(src, dst, send, recv, where):
        return pltpu.make_async_remote_copy(
            src_ref=src, dst_ref=dst, send_sem=send, recv_sem=recv, device_id=where, device_id_type=MESH
        )

    loads = [
        pltpu.make_async_copy(wk_hbm, wk, w_sem.at[0]),
        pltpu.make_async_copy(wv_hbm, wv, w_sem.at[1]),
        pltpu.make_async_copy(wq_hbm, wq, w_sem.at[2]),
    ]
    count = features // cols
    own = [
        pltpu.make_async_copy(tokens_ref.at[pl.ds(j * rp, rp), :], tok.at[line * CHUNKS + j, head], t_sem.at[j])
        for j in range(CHUNKS)
    ]
    for copy in own + loads:
        copy.start()

    barrier = pltpu.get_barrier_semaphore()
    for where in [at_y, at_x, at_c, at_d, at_xy] + [on_line(d) for d in range(1, depth)]:
        pl.semaphore_signal(barrier, inc=1, device_id=where, device_id_type=MESH)

    row_id = lax.broadcasted_iota(jnp.int32, (width, width), 0) // size
    col_id = lax.broadcasted_iota(jnp.int32, (width, width), 1) // size
    mean_mat[...] = jnp.where(row_id == col_id, 1.0 / size, 0.0).astype(BF16)
    acc[...] = jnp.zeros_like(acc)
    pl.semaphore_wait(barrier, 4 + depth)

    def slot_of(n):
        origin, j = visit(line, depth, n)
        return origin, origin * CHUNKS + j

    def z_right(s):
        return remote(tok.at[s, head], tok.at[s, head], zs.at[1, s], zr.at[s], at_right)

    def z_left(s):
        return remote(tok.at[s, head], tok.at[s, head], zs.at[0, s], zr.at[s], at_left)

    def x_copy(s, h):
        return remote(tok.at[s, h], tok.at[s, h], xs.at[s], xr.at[s], at_x)

    def c_copy(s, h, which):
        return remote(tok.at[s, h], tok.at[s, h], cs.at[s, which], cr.at[s, which], at_c)

    def y_copy(s):
        return remote(kvh.at[s, oy], kvr.at[s], ys.at[s], yr.at[s], at_y)

    def q_copy(j):
        return remote(qh.at[oy, j], qr.at[j], qs.at[j], qrs.at[j], at_y)

    def end_copy(d, j):
        away = jnp.where(line == 0, d, depth - d)
        s = line * CHUNKS + j
        return remote(tok.at[s, head], tok.at[s, head], zes.at[d - 1, j], zr.at[s], on_line(away))

    def passes(origin):
        inner = jnp.logical_and(origin > 0, origin < depth - 1)
        right = jnp.logical_and(inner, jnp.logical_and(has_right, origin <= line))
        left = jnp.logical_and(inner, jnp.logical_and(has_left, origin >= line))
        return left, right

    def spread(origin, s):
        left, right = passes(origin)

        @pl.when(right)
        def _():
            z_right(s).start()

        @pl.when(left)
        def _():
            z_left(s).start()

        x_copy(s, head).start()
        c_copy(s, head, 0).start()

    first_far = sorted({1, depth - 1} - {0})
    later_far = [d for d in range(2, depth - 1)]

    for j in range(CHUNKS):
        own[j].wait()
        spread(line, line * CHUNKS + j)

        @pl.when(is_end)
        def _():
            for d in first_far:
                end_copy(d, j).start()

    for copy in loads:
        copy.wait()

    def unit(values):
        mean = jnp.dot((values * values).astype(BF16), mean_mat[...], preferred_element_type=F32)
        return values * lax.rsqrt(mean + EPS)

    lane_w = lax.broadcasted_iota(jnp.int32, (1, width), 1) // size
    scale = jnp.zeros((1, width), F32)
    for h in range(heads):
        scale = jnp.where(lane_w == h, temper_ref[h] * (LOG2E / size), scale)

    def tokens_here(n):
        origin, s = slot_of(n)
        c_copy(s, chead, 0).wait_recv()
        c_copy(s, dhead, 1).wait_recv()

    def project(n):
        origin, s = slot_of(n)
        parts = [tok[s, h].astype(F32) for h in range(count)]
        squares = parts[0] * parts[0]
        for p in parts[1:]:
            squares = squares + p * p
        inv = lax.rsqrt(jnp.sum(squares, axis=-1, keepdims=True) * (1.0 / features) + EPS)
        normed = jnp.concatenate(
            [(parts[h] * inv * gain_ref[:, h * cols:(h + 1) * cols]).astype(BF16) for h in range(count)], axis=1
        )
        keys = unit(jnp.dot(normed, wk[...], preferred_element_type=F32)).astype(BF16)
        values = jnp.dot(normed, wv[...], preferred_element_type=F32).astype(BF16)
        for half in range(2):
            kvh[s, half, 0] = keys[:, half * pair:(half + 1) * pair]
            kvh[s, half, 1] = values[:, half * pair:(half + 1) * pair]
        return normed

    def send_pair(n):
        origin, s = slot_of(n)
        y_copy(s).start()

    def ask(n, normed):
        @pl.when(n < CHUNKS)
        def _():
            query = unit(jnp.dot(normed, wq[...], preferred_element_type=F32))
            query = (query * scale).astype(BF16)
            for half in range(2):
                qh[half, n] = query[:, half * pair:(half + 1) * pair]
            q_copy(n).start()

    low = lax.broadcasted_iota(jnp.int32, (1, pair), 1) < size

    def split_queries():
        for j in range(CHUNKS):
            q_copy(j).wait_recv()
        for side in range(2):
            for j in range(CHUNKS):
                piece = qh[y, j] if side == 0 else qr[j]
                at = side * rows + j * rp
                zero = jnp.zeros_like(piece)
                qm[0, at:at + rp, :] = jnp.where(low, piece, zero)
                qm[1, at:at + rp, :] = jnp.where(low, zero, piece)

    local = rows // BLOCK
    per_chunk = rp // BLOCK
    q_blocks = [order_ref[(line * 2 + side) * local + i] for side in (y, oy) for i in range(local)]
    key_lane = lax.broadcasted_iota(jnp.int32, (1, 2 * rp), 1) // BLOCK

    def pair_here(n):
        origin, s = slot_of(n)
        y_copy(s).wait_recv()

    def fetch(n):
        origin, s = slot_of(n)
        keys = jnp.concatenate([kvh[s, y, 0], kvr[s, 0]], axis=0)
        values = jnp.concatenate([kvh[s, y, 1], kvr[s, 1]], axis=0)
        return keys, values

    def attend(n, keys, values, sides):
        origin, s = slot_of(n)
        first = (s - origin * CHUNKS) * per_chunk
        k_blocks = [order_ref[(origin * 2 + side) * local + first + i] for side in (y, oy) for i in range(per_chunk)]
        masks = []
        for qb in q_blocks:
            mask = jnp.zeros((1, 2 * rp), F32)
            for i, kb in enumerate(k_blocks):
                mask = jnp.where(key_lane == i, (adj_ref[qb, kb] > 0).astype(F32), mask)
            masks.append(mask)
        ones = jnp.ones_like(values)
        at, to = sides[0] * rows, (sides[-1] + 1) * rows
        for h in range(2):
            mine = jnp.where(low, values, ones) if h == 0 else jnp.where(low, ones, values)
            scores = lax.dot_general(qm[h, at:to, :], keys, (((1,), (1,)), ((), ())), preferred_element_type=F32)
            probs = jnp.concatenate(
                [
                    (jnp.exp2(scores[i * BLOCK:(i + 1) * BLOCK]) * masks[at // BLOCK + i]).astype(BF16)
                    for i in range((to - at) // BLOCK)
                ],
                axis=0,
            )
            acc[h, at:to, :] += jnp.dot(probs, mine, preferred_element_type=F32)

    def w_columns(h):
        return wo_hbm.at[:, pl.ds(pl.multiple_of(h * cols, cols), cols)]

    def w_rows(h):
        return wall_ref.at[pl.ds(pl.multiple_of(h * width, width), width), :]

    def w_copy(which):
        h, where = ((xhead, at_x), (dhead, at_d), (chead, at_c))[which]
        return remote(w_columns(h), w_rows(head), ws.at[which], wr.at[which], where)

    def w_own():
        return pltpu.make_async_copy(w_columns(head), w_rows(head), wl)

    def step(n, carry):
        away = n // CHUNKS + 1

        @pl.when(jnp.logical_and(is_end, n == 1))
        def _():
            for d in later_far:
                for j in range(CHUNKS):
                    end_copy(d, j).start()

        @pl.when(line - away >= 0)
        def _():
            s = (line - away) * CHUNKS + n % CHUNKS
            z_right(s).wait_recv()
            spread(line - away, s)

        @pl.when(line + away < depth)
        def _():
            s = (line + away) * CHUNKS + n % CHUNKS
            z_left(s).wait_recv()
            spread(line + away, s)

        @pl.when(n < total)
        def _():
            origin, s = slot_of(n)
            x_copy(s, xhead).wait_recv()
            c_copy(s, xhead, 1).start()

        @pl.when(n == total - 1)
        def _():
            for which in range(3):
                w_copy(which).start()
            w_own().start()

        @pl.when(jnp.logical_or(jnp.logical_and(n >= 1, n < lag), n == total))
        def _():
            tokens_here(n - 1)
            normed = project(n - 1)
            send_pair(n - 1)
            ask(n - 1, normed)

        @pl.when(n == lag)
        def _():
            split_queries()

        @pl.when(jnp.logical_and(n >= lag, n < total))
        def _():
            tokens_here(n - 1)
            pair_here(n - lag)
            keys, values = fetch(n - lag)
            project(n - 1)
            attend(n - lag, keys, values, (0, 1))
            send_pair(n - 1)

        @pl.when(n >= total)
        def _():
            pair_here(n - lag)
            attend(n - lag, *fetch(n - lag), (0, 1))

        return carry

    lax.fori_loop(0, total + lag - 1, step, 0)

    tp = rows // TAIL

    def finish(at):
        first, second = acc[0, at:at + tp, :], acc[1, at:at + tp, :]
        weight = pltpu.roll(jnp.where(low, second, first), size, 1)
        return (jnp.where(low, first, second) / weight).astype(BF16)

    def block(h, half, r):
        at = pl.multiple_of((h * 2 + half) * pair, pair)
        return all_ref.at[pl.ds(r * tp, tp), pl.ds(at, pair)]

    def a_copy(r):
        return remote(asend.at[r], abuf.at[y, r], as_.at[r], ar.at[r], at_y)

    def ax_copy(r):
        return remote(abuf.at[y, r], xbuf.at[y, r], axs.at[0, r], axr.at[0, r], at_x)

    def axy_copy(r):
        return remote(asend.at[r], xbuf.at[y, r], axs.at[1, r], axr.at[1, r], at_xy)

    def ac_copy(src, h, half, r, k):
        return remote(src.at[half, r], block(h, half, r), acs.at[k, r], acr.at[k, r], at_c)

    def keep(src, h, half, r, k):
        return pltpu.make_async_copy(src.at[half, r], block(h, half, r), al.at[k, r])

    pair_here(total - 1)
    keys, values = fetch(total - 1)
    attend(total - 1, keys, values, (1,))
    for r in range(TAIL):
        asend[r] = finish(rows + r * tp)
        axy_copy(r).start()
        a_copy(r).start()
    attend(total - 1, keys, values, (0,))
    for r in range(TAIL):
        abuf[y, r] = finish(r * tp)
        ax_copy(r).start()
    for r in range(TAIL):
        ac_copy(abuf, head, y, r, 0).start()
        keep(abuf, head, y, r, 0).start()

    def drain(n, carry):
        origin, s = slot_of(n)

        left, right = passes(origin)

        @pl.when(right)
        def _():
            z_right(s).wait_send()

        @pl.when(left)
        def _():
            z_left(s).wait_send()

        x_copy(s, head).wait_send()
        c_copy(s, head, 0).wait_send()
        c_copy(s, xhead, 1).wait_send()
        y_copy(s).wait_send()
        return carry

    lax.fori_loop(0, total, drain, 0)

    @pl.when(is_end)
    def _():
        for d in range(1, depth):
            for j in range(CHUNKS):
                end_copy(d, j).wait_send()

    for j in range(CHUNKS):
        q_copy(j).wait_send()
    for r in range(TAIL):
        a_copy(r).wait_recv()
        ac_copy(abuf, head, oy, r, 1).start()
        keep(abuf, head, oy, r, 1).start()
    for r in range(TAIL):
        for k, half, copy in ((1, oy, axy_copy), (0, y, ax_copy)):
            copy(r).wait_recv()
            ac_copy(xbuf, xhead, half, r, 2 + k).start()
            keep(xbuf, xhead, half, r, 2 + k).start()

    for which in range(3):
        w_copy(which).wait()
    w_own().wait()
    for r in range(TAIL):
        a_copy(r).wait_send()
        ax_copy(r).wait_send()
        axy_copy(r).wait_send()
        for k, half in ((0, y), (1, oy)):
            for base, src, h in ((0, abuf, head), (2, xbuf, xhead)):
                ac_copy(src, h, half, r, base + k).wait()
                keep(src, h, half, r, base + k).wait()


def shards(depth, tokens, gain, w_query, w_key, w_value, w_out, temper, adjacency, order):
    rows, cols = tokens.shape
    features, width = w_query.shape
    count = features // cols
    pair = width // 2
    rp = rows // CHUNKS
    tp = rows // TAIL
    total = depth * CHUNKS
    dma = pltpu.SemaphoreType.DMA
    smem = pl.BlockSpec(memory_space=pltpu.SMEM)
    vmem = pl.BlockSpec(memory_space=pltpu.VMEM)
    hbm = pl.BlockSpec(memory_space=pl.ANY)
    attended, weights = pl.pallas_call(
        functools.partial(kernel, depth),
        out_shape=(
            jax.ShapeDtypeStruct((rows, count * width), BF16),
            jax.ShapeDtypeStruct((count * width, cols), BF16),
        ),
        in_specs=[smem, smem, smem, vmem, hbm, hbm, hbm, hbm, hbm],
        out_specs=(hbm, hbm),
        scratch_shapes=[
            pltpu.VMEM((total, count, rp, cols), BF16),
            pltpu.VMEM((features, width), BF16),
            pltpu.VMEM((features, width), BF16),
            pltpu.VMEM((features, width), BF16),
            pltpu.VMEM((width, width), BF16),
            pltpu.VMEM((total, 2, 2, rp, pair), BF16),
            pltpu.VMEM((total, 2, rp, pair), BF16),
            pltpu.VMEM((2, CHUNKS, rp, pair), BF16),
            pltpu.VMEM((CHUNKS, rp, pair), BF16),
            pltpu.VMEM((2, 2 * rows, pair), BF16),
            pltpu.VMEM((2, 2 * rows, pair), F32),
            pltpu.VMEM((TAIL, tp, pair), BF16),
            pltpu.VMEM((2, TAIL, tp, pair), BF16),
            pltpu.VMEM((2, TAIL, tp, pair), BF16),
            dma((3,)),
            dma((CHUNKS,)),
            dma((2, total)),
            dma((max(depth - 1, 1), CHUNKS)),
            dma((total,)),
            dma((total,)),
            dma((total,)),
            dma((total, 2)),
            dma((total, 2)),
            dma((total,)),
            dma((total,)),
            dma((CHUNKS,)),
            dma((CHUNKS,)),
            dma((TAIL,)),
            dma((TAIL,)),
            dma((2, TAIL)),
            dma((2, TAIL)),
            dma((4, TAIL)),
            dma((4, TAIL)),
            dma((4, TAIL)),
            dma((3,)),
            dma((3,)),
            dma,
        ],
        compiler_params=pltpu.CompilerParams(
            collective_id=0, has_side_effects=True, vmem_limit_bytes=56 * 1024 * 1024
        ),
    )(order, adjacency, temper, gain.reshape(1, features), tokens, w_query, w_key, w_value, w_out)
    return jnp.dot(attended, weights, preferred_element_type=F32).astype(BF16)


def solution(mesh):
    in_specs = (
        P("ctx", "head"),
        P(),
        P(None, "head"),
        P(None, "head"),
        P(None, "head"),
        P("head", None),
        P("head"),
        P(),
        P(),
    )
    out_specs = P("ctx", "head")
    body = functools.partial(shards, mesh.shape["ctx"] // 2)
    return jax.shard_map(body, mesh=mesh, in_specs=in_specs, out_specs=out_specs, check_vma=False)
```

```python
import functools

import jax
import jax.numpy as jnp
from jax import lax
from jax.experimental import pallas as pl
from jax.experimental.pallas import tpu as pltpu
from jax.sharding import PartitionSpec as P

BLOCK = 128
CHUNKS = 2
TAIL = 2
EPS = 1e-06
LOG2E = 1.4426950408889634
MESH = pl.DeviceIdType.MESH
F32 = jnp.float32
BF16 = jnp.bfloat16


def visit(line, depth, n):
    far = depth - 1 - line
    near = jnp.minimum(line, far) * CHUNKS
    p = n - CHUNKS
    paired = p < 2 * near
    t = jnp.where(paired, p // 2, p - near)
    to_left = jnp.where(paired, p % 2 == 0, line > far)
    away = t // CHUNKS + 1
    origin = jnp.where(n < CHUNKS, line, jnp.where(to_left, line - away, line + away))
    return origin, jnp.where(n < CHUNKS, n, t % CHUNKS)


def kernel(
    depth,
    order_ref, adj_ref, temper_ref, gain_ref, tokens_ref, wq_hbm, wk_hbm, wv_hbm, wo_hbm,
    all_ref, wall_ref,
    tok, wq, wk, wv, mean_mat, kvh, kvr, qh, qr, qm, acc, asend, abuf, xbuf,
    w_sem, t_sem, zs, zr, xs, xr, cs, cr, ys, yr, qs, qrs, as_, ar, axs, axr, acs, acr, al, ws, wr, wl,
):
    ctx, head = lax.axis_index("ctx"), lax.axis_index("head")
    line, y = ctx // 2, ctx % 2
    x, c = head // 2, head % 2
    oy, ox, oc = 1 - y, 1 - x, 1 - c
    rows, cols = tokens_ref.shape
    heads = temper_ref.shape[0]
    width = wq.shape[1]
    size = width // heads
    pair = width // 2
    rp = rows // CHUNKS
    total = depth * CHUNKS
    features = wq.shape[0]
    lag = CHUNKS + 2
    has_left, has_right = line > 0, line < depth - 1
    at_left, at_right = (ctx - 2, head), (ctx + 2, head)
    at_y = (line * 2 + oy, head)
    at_x = (ctx, ox * 2 + c)
    at_xy = (line * 2 + oy, ox * 2 + c)
    at_c = (ctx, x * 2 + oc)
    xhead = ox * 2 + c
    chead = x * 2 + oc
    dhead = ox * 2 + oc
    at_d = (ctx, dhead)

    def remote(src, dst, send, recv, where):
        return pltpu.make_async_remote_copy(
            src_ref=src, dst_ref=dst, send_sem=send, recv_sem=recv, device_id=where, device_id_type=MESH
        )

    loads = [
        pltpu.make_async_copy(wk_hbm, wk, w_sem.at[0]),
        pltpu.make_async_copy(wv_hbm, wv, w_sem.at[1]),
        pltpu.make_async_copy(wq_hbm, wq, w_sem.at[2]),
    ]
    count = features // cols
    own = [
        pltpu.make_async_copy(tokens_ref.at[pl.ds(j * rp, rp), :], tok.at[line * CHUNKS + j, head], t_sem.at[j])
        for j in range(CHUNKS)
    ]
    barrier = pltpu.get_barrier_semaphore()
    for where in (at_y, at_x, at_c, at_d, at_xy):
        pl.semaphore_signal(barrier, inc=1, device_id=where, device_id_type=MESH)

    @pl.when(has_left)
    def _():
        pl.semaphore_signal(barrier, inc=1, device_id=at_left, device_id_type=MESH)

    @pl.when(has_right)
    def _():
        pl.semaphore_signal(barrier, inc=1, device_id=at_right, device_id_type=MESH)

    for copy in own:
        copy.start()
    pl.semaphore_wait(barrier, 5 + has_left.astype(jnp.int32) + has_right.astype(jnp.int32))

    def slot_of(n):
        origin, j = visit(line, depth, n)
        return origin, origin * CHUNKS + j

    def z_right(s):
        return remote(tok.at[s, head], tok.at[s, head], zs.at[1, s], zr.at[s], at_right)

    def z_left(s):
        return remote(tok.at[s, head], tok.at[s, head], zs.at[0, s], zr.at[s], at_left)

    def x_copy(s, h):
        return remote(tok.at[s, h], tok.at[s, h], xs.at[s], xr.at[s], at_x)

    def c_copy(s, h, which):
        return remote(tok.at[s, h], tok.at[s, h], cs.at[s, which], cr.at[s, which], at_c)

    def y_copy(s):
        return remote(kvh.at[s, oy], kvr.at[s], ys.at[s], yr.at[s], at_y)

    def q_copy(j):
        return remote(qh.at[oy, j], qr.at[j], qs.at[j], qrs.at[j], at_y)

    def spread(origin, s):
        @pl.when(jnp.logical_and(has_right, origin <= line))
        def _():
            z_right(s).start()

        @pl.when(jnp.logical_and(has_left, origin >= line))
        def _():
            z_left(s).start()

        x_copy(s, head).start()
        c_copy(s, head, 0).start()

    for j in range(CHUNKS):
        own[j].wait()
        spread(line, line * CHUNKS + j)
    for copy in loads:
        copy.start()
    row_id = lax.broadcasted_iota(jnp.int32, (width, width), 0) // size
    col_id = lax.broadcasted_iota(jnp.int32, (width, width), 1) // size
    mean_mat[...] = jnp.where(row_id == col_id, 1.0 / size, 0.0).astype(BF16)
    acc[...] = jnp.zeros_like(acc)
    for copy in loads:
        copy.wait()

    def unit(values):
        mean = jnp.dot((values * values).astype(BF16), mean_mat[...], preferred_element_type=F32)
        return values * lax.rsqrt(mean + EPS)

    lane_w = lax.broadcasted_iota(jnp.int32, (1, width), 1) // size
    scale = jnp.zeros((1, width), F32)
    for h in range(heads):
        scale = jnp.where(lane_w == h, temper_ref[h] * (LOG2E / size), scale)

    def tokens_here(n):
        origin, s = slot_of(n)
        c_copy(s, chead, 0).wait_recv()
        c_copy(s, dhead, 1).wait_recv()

    def project(n):
        origin, s = slot_of(n)
        parts = [tok[s, h].astype(F32) for h in range(count)]
        squares = parts[0] * parts[0]
        for p in parts[1:]:
            squares = squares + p * p
        inv = lax.rsqrt(jnp.sum(squares, axis=-1, keepdims=True) * (1.0 / features) + EPS)
        normed = jnp.concatenate(
            [(parts[h] * inv * gain_ref[:, h * cols:(h + 1) * cols]).astype(BF16) for h in range(count)], axis=1
        )
        keys = unit(jnp.dot(normed, wk[...], preferred_element_type=F32)).astype(BF16)
        values = jnp.dot(normed, wv[...], preferred_element_type=F32).astype(BF16)
        for half in range(2):
            kvh[s, half, 0] = keys[:, half * pair:(half + 1) * pair]
            kvh[s, half, 1] = values[:, half * pair:(half + 1) * pair]
        return normed

    def send_pair(n):
        origin, s = slot_of(n)
        y_copy(s).start()

    def ask(n, normed):
        @pl.when(n < CHUNKS)
        def _():
            query = unit(jnp.dot(normed, wq[...], preferred_element_type=F32))
            query = (query * scale).astype(BF16)
            for half in range(2):
                qh[half, n] = query[:, half * pair:(half + 1) * pair]
            q_copy(n).start()

    low = lax.broadcasted_iota(jnp.int32, (1, pair), 1) < size

    def split_queries():
        for j in range(CHUNKS):
            q_copy(j).wait_recv()
        for side in range(2):
            for j in range(CHUNKS):
                piece = qh[y, j] if side == 0 else qr[j]
                at = side * rows + j * rp
                zero = jnp.zeros_like(piece)
                qm[0, at:at + rp, :] = jnp.where(low, piece, zero)
                qm[1, at:at + rp, :] = jnp.where(low, zero, piece)

    local = rows // BLOCK
    per_chunk = rp // BLOCK
    q_blocks = [order_ref[(line * 2 + side) * local + i] for side in (y, oy) for i in range(local)]
    key_lane = lax.broadcasted_iota(jnp.int32, (1, 2 * rp), 1) // BLOCK

    def pair_here(n):
        origin, s = slot_of(n)
        y_copy(s).wait_recv()

    def fetch(n):
        origin, s = slot_of(n)
        keys = jnp.concatenate([kvh[s, y, 0], kvr[s, 0]], axis=0)
        values = jnp.concatenate([kvh[s, y, 1], kvr[s, 1]], axis=0)
        return keys, values

    def attend(n, keys, values, sides):
        origin, s = slot_of(n)
        first = (s - origin * CHUNKS) * per_chunk
        k_blocks = [order_ref[(origin * 2 + side) * local + first + i] for side in (y, oy) for i in range(per_chunk)]
        masks = []
        for qb in q_blocks:
            mask = jnp.zeros((1, 2 * rp), F32)
            for i, kb in enumerate(k_blocks):
                mask = jnp.where(key_lane == i, (adj_ref[qb, kb] > 0).astype(F32), mask)
            masks.append(mask)
        ones = jnp.ones_like(values)
        at, to = sides[0] * rows, (sides[-1] + 1) * rows
        for h in range(2):
            mine = jnp.where(low, values, ones) if h == 0 else jnp.where(low, ones, values)
            scores = lax.dot_general(qm[h, at:to, :], keys, (((1,), (1,)), ((), ())), preferred_element_type=F32)
            probs = jnp.concatenate(
                [
                    (jnp.exp2(scores[i * BLOCK:(i + 1) * BLOCK]) * masks[at // BLOCK + i]).astype(BF16)
                    for i in range((to - at) // BLOCK)
                ],
                axis=0,
            )
            acc[h, at:to, :] += jnp.dot(probs, mine, preferred_element_type=F32)

    def w_columns(h):
        return wo_hbm.at[:, pl.ds(pl.multiple_of(h * cols, cols), cols)]

    def w_rows(h):
        return wall_ref.at[pl.ds(pl.multiple_of(h * width, width), width), :]

    def w_copy(which):
        h, where = ((xhead, at_x), (dhead, at_d), (chead, at_c))[which]
        return remote(w_columns(h), w_rows(head), ws.at[which], wr.at[which], where)

    def w_own():
        return pltpu.make_async_copy(w_columns(head), w_rows(head), wl)

    def step(n, carry):
        @pl.when(n == jnp.where(line == 0, total - 2 * CHUNKS, total - 1))
        def _():
            for which in range(3):
                w_copy(which).start()
            w_own().start()

        away = n // CHUNKS + 1

        @pl.when(line - away >= 0)
        def _():
            s = (line - away) * CHUNKS + n % CHUNKS
            z_right(s).wait_recv()
            spread(line - away, s)

        @pl.when(line + away < depth)
        def _():
            s = (line + away) * CHUNKS + n % CHUNKS
            z_left(s).wait_recv()
            spread(line + away, s)

        @pl.when(n < total)
        def _():
            origin, s = slot_of(n)
            x_copy(s, xhead).wait_recv()
            c_copy(s, xhead, 1).start()

        @pl.when(jnp.logical_or(jnp.logical_and(n >= 1, n < lag), n == total))
        def _():
            tokens_here(n - 1)
            normed = project(n - 1)
            send_pair(n - 1)
            ask(n - 1, normed)

        @pl.when(n == lag)
        def _():
            split_queries()

        @pl.when(jnp.logical_and(n >= lag, n < total))
        def _():
            tokens_here(n - 1)
            pair_here(n - lag)
            keys, values = fetch(n - lag)
            project(n - 1)
            attend(n - lag, keys, values, (0, 1))
            send_pair(n - 1)

        @pl.when(n >= total)
        def _():
            pair_here(n - lag)
            attend(n - lag, *fetch(n - lag), (0, 1))

        return carry

    lax.fori_loop(0, total + lag - 1, step, 0)

    tp = rows // TAIL

    def finish(at):
        first, second = acc[0, at:at + tp, :], acc[1, at:at + tp, :]
        weight = pltpu.roll(jnp.where(low, second, first), size, 1)
        return (jnp.where(low, first, second) / weight).astype(BF16)

    def block(h, half, r):
        at = pl.multiple_of((h * 2 + half) * pair, pair)
        return all_ref.at[pl.ds(r * tp, tp), pl.ds(at, pair)]

    def a_copy(r):
        return remote(asend.at[r], abuf.at[y, r], as_.at[r], ar.at[r], at_y)

    def ax_copy(r):
        return remote(abuf.at[y, r], xbuf.at[y, r], axs.at[0, r], axr.at[0, r], at_x)

    def axy_copy(r):
        return remote(asend.at[r], xbuf.at[y, r], axs.at[1, r], axr.at[1, r], at_xy)

    def ac_copy(src, h, half, r, k):
        return remote(src.at[half, r], block(h, half, r), acs.at[k, r], acr.at[k, r], at_c)

    def keep(src, h, half, r, k):
        return pltpu.make_async_copy(src.at[half, r], block(h, half, r), al.at[k, r])

    pair_here(total - 1)
    keys, values = fetch(total - 1)
    attend(total - 1, keys, values, (1,))
    for r in range(TAIL):
        asend[r] = finish(rows + r * tp)
        axy_copy(r).start()
        a_copy(r).start()
    attend(total - 1, keys, values, (0,))
    for r in range(TAIL):
        abuf[y, r] = finish(r * tp)
        ax_copy(r).start()
    for r in range(TAIL):
        ac_copy(abuf, head, y, r, 0).start()
        keep(abuf, head, y, r, 0).start()

    def drain(n, carry):
        origin, s = slot_of(n)

        @pl.when(jnp.logical_and(has_right, origin <= line))
        def _():
            z_right(s).wait_send()

        @pl.when(jnp.logical_and(has_left, origin >= line))
        def _():
            z_left(s).wait_send()

        x_copy(s, head).wait_send()
        c_copy(s, head, 0).wait_send()
        c_copy(s, xhead, 1).wait_send()
        y_copy(s).wait_send()
        return carry

    lax.fori_loop(0, total, drain, 0)
    for j in range(CHUNKS):
        q_copy(j).wait_send()
    for r in range(TAIL):
        a_copy(r).wait_recv()
        ac_copy(abuf, head, oy, r, 1).start()
        keep(abuf, head, oy, r, 1).start()
    for r in range(TAIL):
        for k, half, copy in ((1, oy, axy_copy), (0, y, ax_copy)):
            copy(r).wait_recv()
            ac_copy(xbuf, xhead, half, r, 2 + k).start()
            keep(xbuf, xhead, half, r, 2 + k).start()

    for which in range(3):
        w_copy(which).wait()
    w_own().wait()
    for r in range(TAIL):
        a_copy(r).wait_send()
        ax_copy(r).wait_send()
        axy_copy(r).wait_send()
        for k, half in ((0, y), (1, oy)):
            for base, src, h in ((0, abuf, head), (2, xbuf, xhead)):
                ac_copy(src, h, half, r, base + k).wait()
                keep(src, h, half, r, base + k).wait()


def shards(depth, tokens, gain, w_query, w_key, w_value, w_out, temper, adjacency, order):
    rows, cols = tokens.shape
    features, width = w_query.shape
    count = features // cols
    pair = width // 2
    rp = rows // CHUNKS
    tp = rows // TAIL
    total = depth * CHUNKS
    dma = pltpu.SemaphoreType.DMA
    smem = pl.BlockSpec(memory_space=pltpu.SMEM)
    vmem = pl.BlockSpec(memory_space=pltpu.VMEM)
    hbm = pl.BlockSpec(memory_space=pl.ANY)
    attended, weights = pl.pallas_call(
        functools.partial(kernel, depth),
        out_shape=(
            jax.ShapeDtypeStruct((rows, count * width), BF16),
            jax.ShapeDtypeStruct((count * width, cols), BF16),
        ),
        in_specs=[smem, smem, smem, vmem, hbm, hbm, hbm, hbm, hbm],
        out_specs=(hbm, hbm),
        scratch_shapes=[
            pltpu.VMEM((total, count, rp, cols), BF16),
            pltpu.VMEM((features, width), BF16),
            pltpu.VMEM((features, width), BF16),
            pltpu.VMEM((features, width), BF16),
            pltpu.VMEM((width, width), BF16),
            pltpu.VMEM((total, 2, 2, rp, pair), BF16),
            pltpu.VMEM((total, 2, rp, pair), BF16),
            pltpu.VMEM((2, CHUNKS, rp, pair), BF16),
            pltpu.VMEM((CHUNKS, rp, pair), BF16),
            pltpu.VMEM((2, 2 * rows, pair), BF16),
            pltpu.VMEM((2, 2 * rows, pair), F32),
            pltpu.VMEM((TAIL, tp, pair), BF16),
            pltpu.VMEM((2, TAIL, tp, pair), BF16),
            pltpu.VMEM((2, TAIL, tp, pair), BF16),
            dma((3,)),
            dma((CHUNKS,)),
            dma((2, total)),
            dma((total,)),
            dma((total,)),
            dma((total,)),
            dma((total, 2)),
            dma((total, 2)),
            dma((total,)),
            dma((total,)),
            dma((CHUNKS,)),
            dma((CHUNKS,)),
            dma((TAIL,)),
            dma((TAIL,)),
            dma((2, TAIL)),
            dma((2, TAIL)),
            dma((4, TAIL)),
            dma((4, TAIL)),
            dma((4, TAIL)),
            dma((3,)),
            dma((3,)),
            dma,
        ],
        compiler_params=pltpu.CompilerParams(
            collective_id=0, has_side_effects=True, vmem_limit_bytes=56 * 1024 * 1024
        ),
    )(order, adjacency, temper, gain.reshape(1, features), tokens, w_query, w_key, w_value, w_out)
    return jnp.dot(attended, weights, preferred_element_type=F32).astype(BF16)


def solution(mesh):
    in_specs = (
        P("ctx", "head"),
        P(),
        P(None, "head"),
        P(None, "head"),
        P(None, "head"),
        P("head", None),
        P("head"),
        P(),
        P(),
    )
    out_specs = P("ctx", "head")
    body = functools.partial(shards, mesh.shape["ctx"] // 2)
    return jax.shard_map(body, mesh=mesh, in_specs=in_specs, out_specs=out_specs, check_vma=False)
```

```python
import functools

import jax
import jax.numpy as jnp
from jax import lax
from jax.experimental import pallas as pl
from jax.experimental.pallas import tpu as pltpu
from jax.sharding import PartitionSpec as P

BLOCK = 128
CHUNKS = 2
TAIL = 2
EPS = 1e-06
LOG2E = 1.4426950408889634
MESH = pl.DeviceIdType.MESH
F32 = jnp.float32
BF16 = jnp.bfloat16


def visit(line, depth, n):
    far = depth - 1 - line
    near = jnp.minimum(line, far) * CHUNKS
    p = n - CHUNKS
    paired = p < 2 * near
    t = jnp.where(paired, p // 2, p - near)
    to_left = jnp.where(paired, p % 2 == 0, line > far)
    away = t // CHUNKS + 1
    origin = jnp.where(n < CHUNKS, line, jnp.where(to_left, line - away, line + away))
    return origin, jnp.where(n < CHUNKS, n, t % CHUNKS)


def group_of(depth):
    return 4 if depth % 4 == 0 else 2 if depth % 2 == 0 else 1


def kernel(
    depth,
    order_ref, adj_ref, temper_ref, gain_ref, tokens_ref, wq_hbm, wk_hbm, wv_hbm, wo_hbm,
    all_ref, wall_ref,
    tok, wq, wk, wv, mean_mat, kvh, kvr, qh, qr, qm, acc, asend, abuf, xbuf,
    w_sem, t_sem, zs, zr, xs, xr, cs, cr, ys, yr, qs, qrs, as_, ar, axs, axr, acs, acr, al, ws, wr, wl, wzs, wzr,
):
    ctx, head = lax.axis_index("ctx"), lax.axis_index("head")
    line, y = ctx // 2, ctx % 2
    x, c = head // 2, head % 2
    oy, ox, oc = 1 - y, 1 - x, 1 - c
    rows, cols = tokens_ref.shape
    heads = temper_ref.shape[0]
    width = wq.shape[1]
    size = width // heads
    pair = width // 2
    rp = rows // CHUNKS
    total = depth * CHUNKS
    features = wq.shape[0]
    lag = CHUNKS + 2
    has_left, has_right = line > 0, line < depth - 1
    at_left, at_right = (ctx - 2, head), (ctx + 2, head)
    at_y = (line * 2 + oy, head)
    at_x = (ctx, ox * 2 + c)
    at_xy = (line * 2 + oy, ox * 2 + c)
    at_c = (ctx, x * 2 + oc)
    xhead = ox * 2 + c
    chead = x * 2 + oc
    dhead = ox * 2 + oc
    at_d = (ctx, dhead)
    group = group_of(depth)
    base, place = line // group * group, line % group
    share = width // group

    def peer(d):
        return ((base + (place + d) % group) * 2 + y, head)


    def remote(src, dst, send, recv, where):
        return pltpu.make_async_remote_copy(
            src_ref=src, dst_ref=dst, send_sem=send, recv_sem=recv, device_id=where, device_id_type=MESH
        )

    loads = [
        pltpu.make_async_copy(wk_hbm, wk, w_sem.at[0]),
        pltpu.make_async_copy(wv_hbm, wv, w_sem.at[1]),
        pltpu.make_async_copy(wq_hbm, wq, w_sem.at[2]),
    ]
    count = features // cols
    own = [
        pltpu.make_async_copy(tokens_ref.at[pl.ds(j * rp, rp), :], tok.at[line * CHUNKS + j, head], t_sem.at[j])
        for j in range(CHUNKS)
    ]
    for copy in own + loads:
        copy.start()

    barrier = pltpu.get_barrier_semaphore()
    for where in (at_y, at_x, at_c, at_d, at_xy):
        pl.semaphore_signal(barrier, inc=1, device_id=where, device_id_type=MESH)

    @pl.when(has_left)
    def _():
        pl.semaphore_signal(barrier, inc=1, device_id=at_left, device_id_type=MESH)

    @pl.when(has_right)
    def _():
        pl.semaphore_signal(barrier, inc=1, device_id=at_right, device_id_type=MESH)

    row_id = lax.broadcasted_iota(jnp.int32, (width, width), 0) // size
    col_id = lax.broadcasted_iota(jnp.int32, (width, width), 1) // size
    mean_mat[...] = jnp.where(row_id == col_id, 1.0 / size, 0.0).astype(BF16)
    acc[...] = jnp.zeros_like(acc)
    pl.semaphore_wait(barrier, 5 + has_left.astype(jnp.int32) + has_right.astype(jnp.int32))

    def slot_of(n):
        origin, j = visit(line, depth, n)
        return origin, origin * CHUNKS + j

    def z_right(s):
        return remote(tok.at[s, head], tok.at[s, head], zs.at[1, s], zr.at[s], at_right)

    def z_left(s):
        return remote(tok.at[s, head], tok.at[s, head], zs.at[0, s], zr.at[s], at_left)

    def x_copy(s, h):
        return remote(tok.at[s, h], tok.at[s, h], xs.at[s], xr.at[s], at_x)

    def c_copy(s, h, which):
        return remote(tok.at[s, h], tok.at[s, h], cs.at[s, which], cr.at[s, which], at_c)

    def y_copy(s):
        return remote(kvh.at[s, oy], kvr.at[s], ys.at[s], yr.at[s], at_y)

    def q_copy(j):
        return remote(qh.at[oy, j], qr.at[j], qs.at[j], qrs.at[j], at_y)

    def spread(origin, s):
        @pl.when(jnp.logical_and(has_right, origin <= line))
        def _():
            z_right(s).start()

        @pl.when(jnp.logical_and(has_left, origin >= line))
        def _():
            z_left(s).start()

        x_copy(s, head).start()
        c_copy(s, head, 0).start()

    for j in range(CHUNKS):
        own[j].wait()
        spread(line, line * CHUNKS + j)
    for copy in loads:
        copy.wait()

    def unit(values):
        mean = jnp.dot((values * values).astype(BF16), mean_mat[...], preferred_element_type=F32)
        return values * lax.rsqrt(mean + EPS)

    lane_w = lax.broadcasted_iota(jnp.int32, (1, width), 1) // size
    scale = jnp.zeros((1, width), F32)
    for h in range(heads):
        scale = jnp.where(lane_w == h, temper_ref[h] * (LOG2E / size), scale)

    def tokens_here(n):
        origin, s = slot_of(n)
        c_copy(s, chead, 0).wait_recv()
        c_copy(s, dhead, 1).wait_recv()

    def project(n):
        origin, s = slot_of(n)
        parts = [tok[s, h].astype(F32) for h in range(count)]
        squares = parts[0] * parts[0]
        for p in parts[1:]:
            squares = squares + p * p
        inv = lax.rsqrt(jnp.sum(squares, axis=-1, keepdims=True) * (1.0 / features) + EPS)
        normed = jnp.concatenate(
            [(parts[h] * inv * gain_ref[:, h * cols:(h + 1) * cols]).astype(BF16) for h in range(count)], axis=1
        )
        keys = unit(jnp.dot(normed, wk[...], preferred_element_type=F32)).astype(BF16)
        values = jnp.dot(normed, wv[...], preferred_element_type=F32).astype(BF16)
        for half in range(2):
            kvh[s, half, 0] = keys[:, half * pair:(half + 1) * pair]
            kvh[s, half, 1] = values[:, half * pair:(half + 1) * pair]
        return normed

    def send_pair(n):
        origin, s = slot_of(n)
        y_copy(s).start()

    def ask(n, normed):
        @pl.when(n < CHUNKS)
        def _():
            query = unit(jnp.dot(normed, wq[...], preferred_element_type=F32))
            query = (query * scale).astype(BF16)
            for half in range(2):
                qh[half, n] = query[:, half * pair:(half + 1) * pair]
            q_copy(n).start()

    low = lax.broadcasted_iota(jnp.int32, (1, pair), 1) < size

    def split_queries():
        for j in range(CHUNKS):
            q_copy(j).wait_recv()
        for side in range(2):
            for j in range(CHUNKS):
                piece = qh[y, j] if side == 0 else qr[j]
                at = side * rows + j * rp
                zero = jnp.zeros_like(piece)
                qm[0, at:at + rp, :] = jnp.where(low, piece, zero)
                qm[1, at:at + rp, :] = jnp.where(low, zero, piece)

    local = rows // BLOCK
    per_chunk = rp // BLOCK
    q_blocks = [order_ref[(line * 2 + side) * local + i] for side in (y, oy) for i in range(local)]
    key_lane = lax.broadcasted_iota(jnp.int32, (1, 2 * rp), 1) // BLOCK

    def pair_here(n):
        origin, s = slot_of(n)
        y_copy(s).wait_recv()

    def fetch(n):
        origin, s = slot_of(n)
        keys = jnp.concatenate([kvh[s, y, 0], kvr[s, 0]], axis=0)
        values = jnp.concatenate([kvh[s, y, 1], kvr[s, 1]], axis=0)
        return keys, values

    def attend(n, keys, values, sides):
        origin, s = slot_of(n)
        first = (s - origin * CHUNKS) * per_chunk
        k_blocks = [order_ref[(origin * 2 + side) * local + first + i] for side in (y, oy) for i in range(per_chunk)]
        masks = []
        for qb in q_blocks:
            mask = jnp.zeros((1, 2 * rp), F32)
            for i, kb in enumerate(k_blocks):
                mask = jnp.where(key_lane == i, (adj_ref[qb, kb] > 0).astype(F32), mask)
            masks.append(mask)
        ones = jnp.ones_like(values)
        at, to = sides[0] * rows, (sides[-1] + 1) * rows
        for h in range(2):
            mine = jnp.where(low, values, ones) if h == 0 else jnp.where(low, ones, values)
            scores = lax.dot_general(qm[h, at:to, :], keys, (((1,), (1,)), ((), ())), preferred_element_type=F32)
            probs = jnp.concatenate(
                [
                    (jnp.exp2(scores[i * BLOCK:(i + 1) * BLOCK]) * masks[at // BLOCK + i]).astype(BF16)
                    for i in range((to - at) // BLOCK)
                ],
                axis=0,
            )
            acc[h, at:to, :] += jnp.dot(probs, mine, preferred_element_type=F32)

    def w_columns(h):
        return wo_hbm.at[:, pl.ds(pl.multiple_of(h * cols, cols), cols)]

    def w_rows(h):
        return wall_ref.at[pl.ds(pl.multiple_of(h * width, width), width), :]

    def w_piece(h, part):
        return wall_ref.at[pl.ds(pl.multiple_of(h * width + part * share, share), share), :]

    def w_copy(which):
        h, where = ((xhead, at_x), (dhead, at_d))[which]
        source = wo_hbm.at[
            pl.ds(pl.multiple_of(place * share, share), share), pl.ds(pl.multiple_of(h * cols, cols), cols)
        ]
        return remote(source, w_piece(head, place), ws.at[which], wr.at[which], where)

    def w_core():
        return remote(w_columns(chead), w_rows(head), ws.at[2], wr.at[2], at_c)

    def w_along(d, which):
        h = (xhead, dhead)[which]
        piece = w_piece(h, place)
        return remote(piece, piece, wzs.at[d - 1, which], wzr.at[d - 1, which], peer(d))

    def w_own():
        return pltpu.make_async_copy(w_columns(head), w_rows(head), wl)

    def step(n, carry):
        away = n // CHUNKS + 1

        @pl.when(line - away >= 0)
        def _():
            s = (line - away) * CHUNKS + n % CHUNKS
            z_right(s).wait_recv()
            spread(line - away, s)

        @pl.when(line + away < depth)
        def _():
            s = (line + away) * CHUNKS + n % CHUNKS
            z_left(s).wait_recv()
            spread(line + away, s)

        @pl.when(n < total)
        def _():
            origin, s = slot_of(n)
            x_copy(s, xhead).wait_recv()
            c_copy(s, xhead, 1).start()

        @pl.when(n == 1)
        def _():
            w_copy(0).start()
            w_copy(1).start()
            w_core().start()
            w_own().start()

        @pl.when(n == total - 2)
        def _():
            for which in range(2):
                w_copy(which).wait_recv()
                for d in range(1, group):
                    w_along(d, which).start()

        @pl.when(jnp.logical_or(jnp.logical_and(n >= 1, n < lag), n == total))
        def _():
            tokens_here(n - 1)
            normed = project(n - 1)
            send_pair(n - 1)
            ask(n - 1, normed)

        @pl.when(n == lag)
        def _():
            split_queries()

        @pl.when(jnp.logical_and(n >= lag, n < total))
        def _():
            tokens_here(n - 1)
            pair_here(n - lag)
            keys, values = fetch(n - lag)
            project(n - 1)
            attend(n - lag, keys, values, (0, 1))
            send_pair(n - 1)

        @pl.when(n >= total)
        def _():
            pair_here(n - lag)
            attend(n - lag, *fetch(n - lag), (0, 1))

        return carry

    lax.fori_loop(0, total + lag - 1, step, 0)

    tp = rows // TAIL

    def finish(at):
        first, second = acc[0, at:at + tp, :], acc[1, at:at + tp, :]
        weight = pltpu.roll(jnp.where(low, second, first), size, 1)
        return (jnp.where(low, first, second) / weight).astype(BF16)

    def block(h, half, r):
        at = pl.multiple_of((h * 2 + half) * pair, pair)
        return all_ref.at[pl.ds(r * tp, tp), pl.ds(at, pair)]

    def a_copy(r):
        return remote(asend.at[r], abuf.at[y, r], as_.at[r], ar.at[r], at_y)

    def ax_copy(r):
        return remote(abuf.at[y, r], xbuf.at[y, r], axs.at[0, r], axr.at[0, r], at_x)

    def axy_copy(r):
        return remote(asend.at[r], xbuf.at[y, r], axs.at[1, r], axr.at[1, r], at_xy)

    def ac_copy(src, h, half, r, k):
        return remote(src.at[half, r], block(h, half, r), acs.at[k, r], acr.at[k, r], at_c)

    def keep(src, h, half, r, k):
        return pltpu.make_async_copy(src.at[half, r], block(h, half, r), al.at[k, r])

    pair_here(total - 1)
    keys, values = fetch(total - 1)
    attend(total - 1, keys, values, (1,))
    for r in range(TAIL):
        asend[r] = finish(rows + r * tp)
        axy_copy(r).start()
        a_copy(r).start()
    attend(total - 1, keys, values, (0,))
    for r in range(TAIL):
        abuf[y, r] = finish(r * tp)
        ax_copy(r).start()
    for r in range(TAIL):
        ac_copy(abuf, head, y, r, 0).start()
        keep(abuf, head, y, r, 0).start()

    def drain(n, carry):
        origin, s = slot_of(n)

        @pl.when(jnp.logical_and(has_right, origin <= line))
        def _():
            z_right(s).wait_send()

        @pl.when(jnp.logical_and(has_left, origin >= line))
        def _():
            z_left(s).wait_send()

        x_copy(s, head).wait_send()
        c_copy(s, head, 0).wait_send()
        c_copy(s, xhead, 1).wait_send()
        y_copy(s).wait_send()
        return carry

    lax.fori_loop(0, total, drain, 0)
    for j in range(CHUNKS):
        q_copy(j).wait_send()
    for r in range(TAIL):
        a_copy(r).wait_recv()
        ac_copy(abuf, head, oy, r, 1).start()
        keep(abuf, head, oy, r, 1).start()
    for r in range(TAIL):
        for k, half, copy in ((1, oy, axy_copy), (0, y, ax_copy)):
            copy(r).wait_recv()
            ac_copy(xbuf, xhead, half, r, 2 + k).start()
            keep(xbuf, xhead, half, r, 2 + k).start()

    for which in range(2):
        w_copy(which).wait_send()
        for d in range(1, group):
            w_along(d, which).wait()
    w_core().wait()
    w_own().wait()
    for r in range(TAIL):
        a_copy(r).wait_send()
        ax_copy(r).wait_send()
        axy_copy(r).wait_send()
        for k, half in ((0, y), (1, oy)):
            for base, src, h in ((0, abuf, head), (2, xbuf, xhead)):
                ac_copy(src, h, half, r, base + k).wait()
                keep(src, h, half, r, base + k).wait()


def shards(depth, tokens, gain, w_query, w_key, w_value, w_out, temper, adjacency, order):
    rows, cols = tokens.shape
    features, width = w_query.shape
    count = features // cols
    pair = width // 2
    rp = rows // CHUNKS
    tp = rows // TAIL
    total = depth * CHUNKS
    dma = pltpu.SemaphoreType.DMA
    smem = pl.BlockSpec(memory_space=pltpu.SMEM)
    vmem = pl.BlockSpec(memory_space=pltpu.VMEM)
    hbm = pl.BlockSpec(memory_space=pl.ANY)
    attended, weights = pl.pallas_call(
        functools.partial(kernel, depth),
        out_shape=(
            jax.ShapeDtypeStruct((rows, count * width), BF16),
            jax.ShapeDtypeStruct((count * width, cols), BF16),
        ),
        in_specs=[smem, smem, smem, vmem, hbm, hbm, hbm, hbm, hbm],
        out_specs=(hbm, hbm),
        scratch_shapes=[
            pltpu.VMEM((total, count, rp, cols), BF16),
            pltpu.VMEM((features, width), BF16),
            pltpu.VMEM((features, width), BF16),
            pltpu.VMEM((features, width), BF16),
            pltpu.VMEM((width, width), BF16),
            pltpu.VMEM((total, 2, 2, rp, pair), BF16),
            pltpu.VMEM((total, 2, rp, pair), BF16),
            pltpu.VMEM((2, CHUNKS, rp, pair), BF16),
            pltpu.VMEM((CHUNKS, rp, pair), BF16),
            pltpu.VMEM((2, 2 * rows, pair), BF16),
            pltpu.VMEM((2, 2 * rows, pair), F32),
            pltpu.VMEM((TAIL, tp, pair), BF16),
            pltpu.VMEM((2, TAIL, tp, pair), BF16),
            pltpu.VMEM((2, TAIL, tp, pair), BF16),
            dma((3,)),
            dma((CHUNKS,)),
            dma((2, total)),
            dma((total,)),
            dma((total,)),
            dma((total,)),
            dma((total, 2)),
            dma((total, 2)),
            dma((total,)),
            dma((total,)),
            dma((CHUNKS,)),
            dma((CHUNKS,)),
            dma((TAIL,)),
            dma((TAIL,)),
            dma((2, TAIL)),
            dma((2, TAIL)),
            dma((4, TAIL)),
            dma((4, TAIL)),
            dma((4, TAIL)),
            dma((3,)),
            dma((3,)),
            dma,
            dma((max(group_of(depth) - 1, 1), 2)),
            dma((max(group_of(depth) - 1, 1), 2)),
        ],
        compiler_params=pltpu.CompilerParams(
            collective_id=0, has_side_effects=True, vmem_limit_bytes=56 * 1024 * 1024
        ),
    )(order, adjacency, temper, gain.reshape(1, features), tokens, w_query, w_key, w_value, w_out)
    return jnp.dot(attended, weights, preferred_element_type=F32).astype(BF16)


def solution(mesh):
    in_specs = (
        P("ctx", "head"),
        P(),
        P(None, "head"),
        P(None, "head"),
        P(None, "head"),
        P("head", None),
        P("head"),
        P(),
        P(),
    )
    out_specs = P("ctx", "head")
    body = functools.partial(shards, mesh.shape["ctx"] // 2)
    return jax.shard_map(body, mesh=mesh, in_specs=in_specs, out_specs=out_specs, check_vma=False)
```

```python
import functools

import jax
import jax.numpy as jnp
from jax import lax
from jax.experimental import pallas as pl
from jax.experimental.pallas import tpu as pltpu
from jax.sharding import PartitionSpec as P

BLOCK = 128
CHUNKS = 2
TAIL = 2
EPS = 1e-06
LOG2E = 1.4426950408889634
MESH = pl.DeviceIdType.MESH
F32 = jnp.float32
BF16 = jnp.bfloat16


def visit(line, depth, n):
    far = depth - 1 - line
    near = jnp.minimum(line, far) * CHUNKS
    p = n - CHUNKS
    paired = p < 2 * near
    t = jnp.where(paired, p // 2, p - near)
    to_left = jnp.where(paired, p % 2 == 0, line > far)
    away = t // CHUNKS + 1
    origin = jnp.where(n < CHUNKS, line, jnp.where(to_left, line - away, line + away))
    return origin, jnp.where(n < CHUNKS, n, t % CHUNKS)


def group_of(depth):
    return 4 if depth % 4 == 0 else 2 if depth % 2 == 0 else 1


def kernel(
    depth,
    order_ref, adj_ref, temper_ref, gain_ref, tokens_ref, wq_hbm, wk_hbm, wv_hbm, wo_hbm,
    all_ref, wall_ref,
    tok, wq, wk, wv, mean_mat, kvh, kvr, qh, qr, qm, acc, asend, abuf, xbuf,
    w_sem, t_sem, zs, zr, xs, xr, cs, cr, ys, yr, qs, qrs, as_, ar, axs, axr, acs, acr, al, ws, wr, wl, wzs, wzr,
):
    ctx, head = lax.axis_index("ctx"), lax.axis_index("head")
    line, y = ctx // 2, ctx % 2
    x, c = head // 2, head % 2
    oy, ox, oc = 1 - y, 1 - x, 1 - c
    rows, cols = tokens_ref.shape
    heads = temper_ref.shape[0]
    width = wq.shape[1]
    size = width // heads
    pair = width // 2
    rp = rows // CHUNKS
    total = depth * CHUNKS
    features = wq.shape[0]
    lag = CHUNKS + 2
    has_left, has_right = line > 0, line < depth - 1
    at_left, at_right = (ctx - 2, head), (ctx + 2, head)
    at_y = (line * 2 + oy, head)
    at_x = (ctx, ox * 2 + c)
    at_xy = (line * 2 + oy, ox * 2 + c)
    at_c = (ctx, x * 2 + oc)
    xhead = ox * 2 + c
    chead = x * 2 + oc
    dhead = ox * 2 + oc
    at_d = (ctx, dhead)
    group = group_of(depth)
    base, place = line // group * group, line % group
    share = width // group

    def peer(d):
        return ((base + (place + d) % group) * 2 + y, head)


    def remote(src, dst, send, recv, where):
        return pltpu.make_async_remote_copy(
            src_ref=src, dst_ref=dst, send_sem=send, recv_sem=recv, device_id=where, device_id_type=MESH
        )

    loads = [
        pltpu.make_async_copy(wk_hbm, wk, w_sem.at[0]),
        pltpu.make_async_copy(wv_hbm, wv, w_sem.at[1]),
        pltpu.make_async_copy(wq_hbm, wq, w_sem.at[2]),
    ]
    count = features // cols
    own = [
        pltpu.make_async_copy(tokens_ref.at[pl.ds(j * rp, rp), :], tok.at[line * CHUNKS + j, head], t_sem.at[j])
        for j in range(CHUNKS)
    ]
    for copy in own + loads:
        copy.start()

    barrier = pltpu.get_barrier_semaphore()
    for where in (at_y, at_x, at_c, at_d, at_xy):
        pl.semaphore_signal(barrier, inc=1, device_id=where, device_id_type=MESH)

    @pl.when(has_left)
    def _():
        pl.semaphore_signal(barrier, inc=1, device_id=at_left, device_id_type=MESH)

    @pl.when(has_right)
    def _():
        pl.semaphore_signal(barrier, inc=1, device_id=at_right, device_id_type=MESH)

    row_id = lax.broadcasted_iota(jnp.int32, (width, width), 0) // size
    col_id = lax.broadcasted_iota(jnp.int32, (width, width), 1) // size
    mean_mat[...] = jnp.where(row_id == col_id, 1.0 / size, 0.0).astype(BF16)
    acc[...] = jnp.zeros_like(acc)
    pl.semaphore_wait(barrier, 5 + has_left.astype(jnp.int32) + has_right.astype(jnp.int32))

    def slot_of(n):
        origin, j = visit(line, depth, n)
        return origin, origin * CHUNKS + j

    def z_right(s):
        return remote(tok.at[s, head], tok.at[s, head], zs.at[1, s], zr.at[s], at_right)

    def z_left(s):
        return remote(tok.at[s, head], tok.at[s, head], zs.at[0, s], zr.at[s], at_left)

    def x_copy(s, h):
        return remote(tok.at[s, h], tok.at[s, h], xs.at[s], xr.at[s], at_x)

    def c_copy(s, h, which):
        return remote(tok.at[s, h], tok.at[s, h], cs.at[s, which], cr.at[s, which], at_c)

    def y_copy(s):
        return remote(kvh.at[s, oy], kvr.at[s], ys.at[s], yr.at[s], at_y)

    def q_copy(j):
        return remote(qh.at[oy, j], qr.at[j], qs.at[j], qrs.at[j], at_y)

    def spread(origin, s):
        @pl.when(jnp.logical_and(has_right, origin <= line))
        def _():
            z_right(s).start()

        @pl.when(jnp.logical_and(has_left, origin >= line))
        def _():
            z_left(s).start()

        x_copy(s, head).start()
        c_copy(s, head, 0).start()

    for j in range(CHUNKS):
        own[j].wait()
        spread(line, line * CHUNKS + j)
    for copy in loads:
        copy.wait()

    def unit(values):
        mean = jnp.dot((values * values).astype(BF16), mean_mat[...], preferred_element_type=F32)
        return values * lax.rsqrt(mean + EPS)

    lane_w = lax.broadcasted_iota(jnp.int32, (1, width), 1) // size
    scale = jnp.zeros((1, width), F32)
    for h in range(heads):
        scale = jnp.where(lane_w == h, temper_ref[h] * (LOG2E / size), scale)

    def tokens_here(n):
        origin, s = slot_of(n)
        c_copy(s, chead, 0).wait_recv()
        c_copy(s, dhead, 1).wait_recv()

    def project(n):
        origin, s = slot_of(n)
        parts = [tok[s, h].astype(F32) for h in range(count)]
        squares = parts[0] * parts[0]
        for p in parts[1:]:
            squares = squares + p * p
        inv = lax.rsqrt(jnp.sum(squares, axis=-1, keepdims=True) * (1.0 / features) + EPS)
        normed = jnp.concatenate(
            [(parts[h] * inv * gain_ref[:, h * cols:(h + 1) * cols]).astype(BF16) for h in range(count)], axis=1
        )
        keys = unit(jnp.dot(normed, wk[...], preferred_element_type=F32)).astype(BF16)
        values = jnp.dot(normed, wv[...], preferred_element_type=F32).astype(BF16)
        for half in range(2):
            kvh[s, half, 0] = keys[:, half * pair:(half + 1) * pair]
            kvh[s, half, 1] = values[:, half * pair:(half + 1) * pair]
        return normed

    def send_pair(n):
        origin, s = slot_of(n)
        y_copy(s).start()

    def ask(n, normed):
        @pl.when(n < CHUNKS)
        def _():
            query = unit(jnp.dot(normed, wq[...], preferred_element_type=F32))
            query = (query * scale).astype(BF16)
            for half in range(2):
                qh[half, n] = query[:, half * pair:(half + 1) * pair]
            q_copy(n).start()

    low = lax.broadcasted_iota(jnp.int32, (1, pair), 1) < size

    def split_queries():
        for j in range(CHUNKS):
            q_copy(j).wait_recv()
        for side in range(2):
            for j in range(CHUNKS):
                piece = qh[y, j] if side == 0 else qr[j]
                at = side * rows + j * rp
                zero = jnp.zeros_like(piece)
                qm[0, at:at + rp, :] = jnp.where(low, piece, zero)
                qm[1, at:at + rp, :] = jnp.where(low, zero, piece)

    local = rows // BLOCK
    per_chunk = rp // BLOCK
    q_blocks = [order_ref[(line * 2 + side) * local + i] for side in (y, oy) for i in range(local)]
    key_lane = lax.broadcasted_iota(jnp.int32, (1, 2 * rp), 1) // BLOCK

    def pair_here(n):
        origin, s = slot_of(n)
        y_copy(s).wait_recv()

    def fetch(n):
        origin, s = slot_of(n)
        keys = jnp.concatenate([kvh[s, y, 0], kvr[s, 0]], axis=0)
        values = jnp.concatenate([kvh[s, y, 1], kvr[s, 1]], axis=0)
        return keys, values

    def attend(n, keys, values, sides):
        origin, s = slot_of(n)
        first = (s - origin * CHUNKS) * per_chunk
        k_blocks = [order_ref[(origin * 2 + side) * local + first + i] for side in (y, oy) for i in range(per_chunk)]
        masks = []
        for qb in q_blocks:
            mask = jnp.zeros((1, 2 * rp), F32)
            for i, kb in enumerate(k_blocks):
                mask = jnp.where(key_lane == i, (adj_ref[qb, kb] > 0).astype(F32), mask)
            masks.append(mask)
        ones = jnp.ones_like(values)
        at, to = sides[0] * rows, (sides[-1] + 1) * rows
        for h in range(2):
            mine = jnp.where(low, values, ones) if h == 0 else jnp.where(low, ones, values)
            scores = lax.dot_general(qm[h, at:to, :], keys, (((1,), (1,)), ((), ())), preferred_element_type=F32)
            probs = jnp.concatenate(
                [
                    (jnp.exp2(scores[i * BLOCK:(i + 1) * BLOCK]) * masks[at // BLOCK + i]).astype(BF16)
                    for i in range((to - at) // BLOCK)
                ],
                axis=0,
            )
            acc[h, at:to, :] += jnp.dot(probs, mine, preferred_element_type=F32)

    def w_columns(h):
        return wo_hbm.at[:, pl.ds(pl.multiple_of(h * cols, cols), cols)]

    def w_rows(h):
        return wall_ref.at[pl.ds(pl.multiple_of(h * width, width), width), :]

    def w_piece(h, part):
        return wall_ref.at[pl.ds(pl.multiple_of(h * width + part * share, share), share), :]

    def w_copy(which):
        h, where = ((xhead, at_x), (dhead, at_d))[which]
        source = wo_hbm.at[
            pl.ds(pl.multiple_of(place * share, share), share), pl.ds(pl.multiple_of(h * cols, cols), cols)
        ]
        return remote(source, w_piece(head, place), ws.at[which], wr.at[which], where)

    def w_core():
        return remote(w_columns(chead), w_rows(head), ws.at[2], wr.at[2], at_c)

    def w_along(d, which):
        h = (xhead, dhead)[which]
        piece = w_piece(h, place)
        return remote(piece, piece, wzs.at[d - 1, which], wzr.at[d - 1, which], peer(d))

    def w_own():
        return pltpu.make_async_copy(w_columns(head), w_rows(head), wl)

    def step(n, carry):
        away = n // CHUNKS + 1

        @pl.when(line - away >= 0)
        def _():
            s = (line - away) * CHUNKS + n % CHUNKS
            z_right(s).wait_recv()
            spread(line - away, s)

        @pl.when(line + away < depth)
        def _():
            s = (line + away) * CHUNKS + n % CHUNKS
            z_left(s).wait_recv()
            spread(line + away, s)

        @pl.when(n < total)
        def _():
            origin, s = slot_of(n)
            x_copy(s, xhead).wait_recv()
            c_copy(s, xhead, 1).start()

        @pl.when(n == total - 2)
        def _():
            w_copy(0).start()
            w_copy(1).start()

        @pl.when(jnp.logical_or(jnp.logical_and(n >= 1, n < lag), n == total))
        def _():
            tokens_here(n - 1)
            normed = project(n - 1)
            send_pair(n - 1)
            ask(n - 1, normed)

        @pl.when(n == lag)
        def _():
            split_queries()

        @pl.when(jnp.logical_and(n >= lag, n < total))
        def _():
            tokens_here(n - 1)
            pair_here(n - lag)
            keys, values = fetch(n - lag)
            project(n - 1)
            attend(n - lag, keys, values, (0, 1))
            send_pair(n - 1)

        @pl.when(n == total)
        def _():
            w_core().start()
            w_own().start()
            for which in range(2):
                w_copy(which).wait_recv()
                for d in range(1, group):
                    w_along(d, which).start()

        @pl.when(n >= total)
        def _():
            pair_here(n - lag)
            attend(n - lag, *fetch(n - lag), (0, 1))

        return carry

    lax.fori_loop(0, total + lag - 1, step, 0)

    tp = rows // TAIL

    def finish(at):
        first, second = acc[0, at:at + tp, :], acc[1, at:at + tp, :]
        weight = pltpu.roll(jnp.where(low, second, first), size, 1)
        return (jnp.where(low, first, second) / weight).astype(BF16)

    def block(h, half, r):
        at = pl.multiple_of((h * 2 + half) * pair, pair)
        return all_ref.at[pl.ds(r * tp, tp), pl.ds(at, pair)]

    def a_copy(r):
        return remote(asend.at[r], abuf.at[y, r], as_.at[r], ar.at[r], at_y)

    def ax_copy(r):
        return remote(abuf.at[y, r], xbuf.at[y, r], axs.at[0, r], axr.at[0, r], at_x)

    def axy_copy(r):
        return remote(asend.at[r], xbuf.at[y, r], axs.at[1, r], axr.at[1, r], at_xy)

    def ac_copy(src, h, half, r, k):
        return remote(src.at[half, r], block(h, half, r), acs.at[k, r], acr.at[k, r], at_c)

    def keep(src, h, half, r, k):
        return pltpu.make_async_copy(src.at[half, r], block(h, half, r), al.at[k, r])

    pair_here(total - 1)
    keys, values = fetch(total - 1)
    attend(total - 1, keys, values, (1,))
    for r in range(TAIL):
        asend[r] = finish(rows + r * tp)
        axy_copy(r).start()
        a_copy(r).start()
    attend(total - 1, keys, values, (0,))
    for r in range(TAIL):
        abuf[y, r] = finish(r * tp)
        ax_copy(r).start()
    for r in range(TAIL):
        ac_copy(abuf, head, y, r, 0).start()
        keep(abuf, head, y, r, 0).start()

    def drain(n, carry):
        origin, s = slot_of(n)

        @pl.when(jnp.logical_and(has_right, origin <= line))
        def _():
            z_right(s).wait_send()

        @pl.when(jnp.logical_and(has_left, origin >= line))
        def _():
            z_left(s).wait_send()

        x_copy(s, head).wait_send()
        c_copy(s, head, 0).wait_send()
        c_copy(s, xhead, 1).wait_send()
        y_copy(s).wait_send()
        return carry

    lax.fori_loop(0, total, drain, 0)
    for j in range(CHUNKS):
        q_copy(j).wait_send()
    for r in range(TAIL):
        a_copy(r).wait_recv()
        ac_copy(abuf, head, oy, r, 1).start()
        keep(abuf, head, oy, r, 1).start()
    for r in range(TAIL):
        for k, half, copy in ((1, oy, axy_copy), (0, y, ax_copy)):
            copy(r).wait_recv()
            ac_copy(xbuf, xhead, half, r, 2 + k).start()
            keep(xbuf, xhead, half, r, 2 + k).start()

    for which in range(2):
        w_copy(which).wait_send()
        for d in range(1, group):
            w_along(d, which).wait()
    w_core().wait()
    w_own().wait()
    for r in range(TAIL):
        a_copy(r).wait_send()
        ax_copy(r).wait_send()
        axy_copy(r).wait_send()
        for k, half in ((0, y), (1, oy)):
            for base, src, h in ((0, abuf, head), (2, xbuf, xhead)):
                ac_copy(src, h, half, r, base + k).wait()
                keep(src, h, half, r, base + k).wait()


def shards(depth, tokens, gain, w_query, w_key, w_value, w_out, temper, adjacency, order):
    rows, cols = tokens.shape
    features, width = w_query.shape
    count = features // cols
    pair = width // 2
    rp = rows // CHUNKS
    tp = rows // TAIL
    total = depth * CHUNKS
    dma = pltpu.SemaphoreType.DMA
    smem = pl.BlockSpec(memory_space=pltpu.SMEM)
    vmem = pl.BlockSpec(memory_space=pltpu.VMEM)
    hbm = pl.BlockSpec(memory_space=pl.ANY)
    attended, weights = pl.pallas_call(
        functools.partial(kernel, depth),
        out_shape=(
            jax.ShapeDtypeStruct((rows, count * width), BF16),
            jax.ShapeDtypeStruct((count * width, cols), BF16),
        ),
        in_specs=[smem, smem, smem, vmem, hbm, hbm, hbm, hbm, hbm],
        out_specs=(hbm, hbm),
        scratch_shapes=[
            pltpu.VMEM((total, count, rp, cols), BF16),
            pltpu.VMEM((features, width), BF16),
            pltpu.VMEM((features, width), BF16),
            pltpu.VMEM((features, width), BF16),
            pltpu.VMEM((width, width), BF16),
            pltpu.VMEM((total, 2, 2, rp, pair), BF16),
            pltpu.VMEM((total, 2, rp, pair), BF16),
            pltpu.VMEM((2, CHUNKS, rp, pair), BF16),
            pltpu.VMEM((CHUNKS, rp, pair), BF16),
            pltpu.VMEM((2, 2 * rows, pair), BF16),
            pltpu.VMEM((2, 2 * rows, pair), F32),
            pltpu.VMEM((TAIL, tp, pair), BF16),
            pltpu.VMEM((2, TAIL, tp, pair), BF16),
            pltpu.VMEM((2, TAIL, tp, pair), BF16),
            dma((3,)),
            dma((CHUNKS,)),
            dma((2, total)),
            dma((total,)),
            dma((total,)),
            dma((total,)),
            dma((total, 2)),
            dma((total, 2)),
            dma((total,)),
            dma((total,)),
            dma((CHUNKS,)),
            dma((CHUNKS,)),
            dma((TAIL,)),
            dma((TAIL,)),
            dma((2, TAIL)),
            dma((2, TAIL)),
            dma((4, TAIL)),
            dma((4, TAIL)),
            dma((4, TAIL)),
            dma((3,)),
            dma((3,)),
            dma,
            dma((max(group_of(depth) - 1, 1), 2)),
            dma((max(group_of(depth) - 1, 1), 2)),
        ],
        compiler_params=pltpu.CompilerParams(
            collective_id=0, has_side_effects=True, vmem_limit_bytes=56 * 1024 * 1024
        ),
    )(order, adjacency, temper, gain.reshape(1, features), tokens, w_query, w_key, w_value, w_out)
    return jnp.dot(attended, weights, preferred_element_type=F32).astype(BF16)


def solution(mesh):
    in_specs = (
        P("ctx", "head"),
        P(),
        P(None, "head"),
        P(None, "head"),
        P(None, "head"),
        P("head", None),
        P("head"),
        P(),
        P(),
    )
    out_specs = P("ctx", "head")
    body = functools.partial(shards, mesh.shape["ctx"] // 2)
    return jax.shard_map(body, mesh=mesh, in_specs=in_specs, out_specs=out_specs, check_vma=False)
```
